32 devices in a mesh: ens: 2 (over x), cells: 16 (over z, y, core).
Axes of the slice: x: 2, y: 2, z: 4, core: 2. Of those that a mesh axis runs over, the one named last changes fastest.
Arguments:
- control: float32 [64, 128, 2048], P('ens', 'cells'), parts along dimension 0
- prior_flux: float32 [32, 128, 2048], P(None, 'cells'), may hold values from -6 to 6
- area_weight: float32 [128, 2048], P('cells')
- time_factor: float32 [32, 32], replicated
- lat_factor: float32 [128, 128], replicated
- coarse_lon: float32 [16, 16], replicated
- fine_lon: float32 [128, 128], replicated
- footprint_tiles: int32 [2048, 8], P('cells'), may hold values from 0 to 2047, as said below
- footprint_hours: int32 [2048, 8], P('cells'), may hold values from 0 to 31
- footprint_weights: bfloat16 [2048, 8, 128], P('cells'), may hold values from -0.09472656 to 0.10498047
- observations: float32 [4096], P(('ens', 'cells')), parts along dimension 0, may hold values from -4 to 0
- error_variance: float32 [2048], P('cells'), may hold values from 0.5 to 4
Outputs:
- gradient: float32 [64, 128, 2048], P('ens', 'cells'), parts along dimension 0
- misfit: float32 [4096], P(('ens', 'cells')), parts along dimension 0
The draws below stay inside these ranges and needn't reach their ends.
There are 2 independent parts, one for each index of `ens`. The reference program is written for one: setup_inputs(seed, part) draws one part's arguments, and reference() takes and returns one part's arrays. A program takes and returns all parts, laid end to end along the dimension named above; an argument that names none is the same for every part. Nothing has to cross between parts.
Inputs may be any that keep to these rules, and one draw needn't show every extreme that they name: A tile's cells belong to device footprint_tiles // 128. The slots of one device's soundings name tiles of any one device at most 128 times, and exactly 128 times for some device.
All inputs are finite; a program needn't handle non-finite values.
Results may differ from the reference program's by a relative error of at most 0.0021.
Values may be sent and summed in bfloat16 or wider, within the bound.
A program may use at most 128 MiB of HBM per device.

```python
import math
import jax
import jax.numpy as jnp
from jax import lax

HOURS = 32
LON = 2048
TILE_CELLS = 128
FOOT = 8
LATD = 8
S_DEV = 128
LAT = 128
LONC = 16
TILES_DEV = 128
SOUNDINGS = 2048
N_CELLS = 16


def correlation_root(key, extent, length, mix_low, mix_high, noise_level):
    key_mix, key_noise = jax.random.split(key)
    position = jnp.arange(extent, dtype=jnp.float32)
    distance = jnp.abs(position[:, None] - position[None, :])
    smooth = jnp.exp(-distance / length) / length
    mixing = jax.random.uniform(key_mix, (extent, extent), jnp.float32, mix_low, mix_high)
    scatter = jax.random.normal(key_noise, (extent, extent), jnp.float32) * (noise_level / math.sqrt(extent))
    return (smooth * mixing + scatter).astype(jnp.float32)


def draw_control(key, part):
    key = jax.random.fold_in(key, 37)
    key_offset, key_noise = jax.random.split(key)
    offsets = jax.random.uniform(key_offset, (HOURS,), jnp.float32, 0.01, 0.05)
    noise = 0.3 * jax.random.normal(key_noise, (HOURS, LAT, LON), jnp.float32)
    return (offsets[:, None, None] + noise).astype(jnp.float32)


def draw_time_factor(key, part):
    key = jax.random.fold_in(key, 17)
    return correlation_root(key, HOURS, HOURS / 4.0, 0.5, 1.5, 1.0)


def draw_lat_factor(key, part):
    key = jax.random.fold_in(key, 23)
    latitude = jnp.arange(LAT, dtype=jnp.float32) / max(LAT - 1, 1)
    rising = 1.0 + 2.0 * latitude
    root = correlation_root(key, LAT, 8.0 * LATD, 0.5, 1.5, 1.0)
    return (rising[:, None] * root).astype(jnp.float32)


def draw_coarse_lon(key, part):
    key = jax.random.fold_in(key, 29)
    key_root, key_rows = jax.random.split(key)
    scales = jnp.exp(jax.random.uniform(key_rows, (LONC,), jnp.float32, 0.0, math.log(3.0)))
    root = correlation_root(key_root, LONC, max(LONC / 4.0, 1.0), 0.5, 1.5, 1.0)
    return (scales[:, None] * root).astype(jnp.float32)


def draw_fine_lon(key, part):
    key = jax.random.fold_in(key, 31)
    return correlation_root(key, TILE_CELLS, TILE_CELLS / 8.0, 0.5, 1.5, 1.0)


def draw_area_weight(key, part):
    key = jax.random.fold_in(key, 5)
    latitude = jnp.arange(LAT, dtype=jnp.float32)
    rising = 1.0 + 2.0 * latitude / max(LAT - 1, 1)
    spread = jnp.exp(jax.random.uniform(key, (LAT, LON), jnp.float32, jnp.log(0.5), jnp.log(2.0)))
    return (rising[:, None] * spread).astype(jnp.float32)


def draw_footprint_tiles(key, part):
    key = jax.random.fold_in(key, 11)
    blocks = N_CELLS
    slot_total = S_DEV * FOOT
    average = slot_total // blocks
    quarter = blocks // 4
    first_part = quarter * 2 * average

    def one_device(device_key):
        key_shift, key_order, key_local = jax.random.split(device_key, 3)
        offset = jax.random.randint(key_shift, (), 0, blocks)
        places = jnp.arange(slot_total, dtype=jnp.int32)
        relative = jnp.where(places < first_part, places // (2 * average), quarter + (places - first_part) // average)
        owners = (relative + offset) % blocks
        owners = owners[jax.random.permutation(key_order, slot_total)]
        within = jax.random.randint(key_local, (slot_total,), 0, TILES_DEV)
        return (owners * TILES_DEV + within).astype(jnp.int32).reshape(S_DEV, FOOT)
    device_keys = jax.random.split(key, blocks)
    return jax.vmap(one_device)(device_keys).reshape(S_DEV * blocks, FOOT)


def touch_ends(values, key, low, largest):
    longest = values.shape.index(max(values.shape))
    spots = []
    for shift in (0, 1):
        where = [jax.random.randint(jax.random.fold_in(key, axis), (), 0, length) for axis, length in enumerate(values.shape)]
        where[longest] = (where[longest] + shift) % values.shape[longest]
        spots.append(tuple(where))
    return values.at[spots[0]].set(low).at[spots[1]].set(largest)


def shard_levels(key, shape, pieces, low, high):
    def one(axis_at, shards_of):
        steps = jax.random.uniform(jax.random.fold_in(jax.random.fold_in(key, 6), axis_at), (shards_of,), jnp.float32, low / len(pieces), high / len(pieces))
        return jnp.repeat(jnp.exp(steps), shape[axis_at] // shards_of).reshape((-1,) + (1,) * (len(shape) - axis_at - 1))

    gain = one(*pieces[0])
    for cut in pieces[1:]:
        gain = gain * one(*cut)
    return gain


def normal_values(rng, shape, scale, limit, shards=(), kind=jnp.bfloat16):
    array = scale * jax.random.normal(rng, shape, jnp.float32)
    if shards:
        array = array * shard_levels(rng, shape, shards, -0.22, 0.18)
    return jnp.clip(array, -limit, limit).astype(kind)


def setup_inputs(seed: int = 0, part: int = 0) -> dict:
    splits = jax.random.split(jax.random.key(seed), 13)
    own_keys = jax.random.split(jax.random.fold_in(splits[12], part), 13)
    control = draw_control(jax.random.fold_in(jax.random.fold_in(splits[12], part), 71), part)
    prior_flux = normal_values(splits[1], (HOURS, LAT, LON), 1.0, 6.0, ((1, 16),), jnp.float32)
    area_weight = draw_area_weight(jax.random.fold_in(splits[12], 71), part)
    time_factor = draw_time_factor(jax.random.fold_in(splits[12], 71), part)
    lat_factor = draw_lat_factor(jax.random.fold_in(splits[12], 71), part)
    coarse_lon = draw_coarse_lon(jax.random.fold_in(splits[12], 71), part)
    fine_lon = draw_fine_lon(jax.random.fold_in(splits[12], 71), part)
    footprint_tiles = draw_footprint_tiles(jax.random.fold_in(splits[12], 71), part)
    footprint_hours = touch_ends(jax.random.randint(splits[8], (SOUNDINGS, FOOT), 0, HOURS), jax.random.fold_in(splits[8], 1), 0, HOURS - 1).astype(jnp.int32)
    footprint_weights = jnp.clip(-0.09472656 + 0.19970703 * jax.random.uniform(splits[9], (SOUNDINGS, FOOT, TILE_CELLS), jnp.float32) ** shard_levels(splits[9], (SOUNDINGS, FOOT, TILE_CELLS), ((0, 16),), -0.2, 0.2), -0.09472656, 0.10498047).astype(jnp.bfloat16)
    observations = jnp.clip(-4.0 + 4.0 * jax.random.uniform(own_keys[10], (SOUNDINGS,), jnp.float32) ** shard_levels(own_keys[10], (SOUNDINGS,), ((0, 16),), -0.2, 0.2), -4.0, 0.0)
    error_variance = jnp.clip(jnp.exp(math.log(4.0) - 2.0794415 * jax.random.uniform(splits[11], (SOUNDINGS,), jnp.float32) ** shard_levels(splits[11], (SOUNDINGS,), ((0, 16),), -0.2, 0.2)), 0.5, 4.0)
    return dict(control=control, prior_flux=prior_flux, area_weight=area_weight, time_factor=time_factor, lat_factor=lat_factor, coarse_lon=coarse_lon, fine_lon=fine_lon, footprint_tiles=footprint_tiles, footprint_hours=footprint_hours, footprint_weights=footprint_weights, observations=observations, error_variance=error_variance)


highest = lax.Precision.HIGHEST


def lon_apply(field, coarse_lon, fine_lon):
    shaped = field.reshape(field.shape[0], field.shape[1], coarse_lon.shape[0], fine_lon.shape[0])
    shaped = jnp.einsum('hapq,fq->hapf', shaped, fine_lon, precision=highest)
    shaped = jnp.einsum('hapf,cp->hacf', shaped, coarse_lon, precision=highest)
    return shaped.reshape(field.shape)


def lon_adjoint(field, coarse_lon, fine_lon):
    shaped = field.reshape(field.shape[0], field.shape[1], coarse_lon.shape[0], fine_lon.shape[0])
    shaped = jnp.einsum('hapq,qf->hapf', shaped, fine_lon, precision=highest)
    shaped = jnp.einsum('hapf,pc->hacf', shaped, coarse_lon, precision=highest)
    return shaped.reshape(field.shape)


def time_apply(field, time_factor):
    return jnp.einsum('gh,hab->gab', time_factor, field, precision=highest)


def time_adjoint(field, time_factor):
    return jnp.einsum('hg,hab->gab', time_factor, field, precision=highest)


def lat_apply(field, lat_factor):
    return jnp.einsum('ca,hab->hcb', lat_factor, field, precision=highest)


def lat_adjoint(field, lat_factor):
    return jnp.einsum('ac,hab->hcb', lat_factor, field, precision=highest)


def reference(control, prior_flux, area_weight, time_factor, lat_factor, coarse_lon, fine_lon, footprint_tiles, footprint_hours, footprint_weights, observations, error_variance):
    increment = lat_apply(time_apply(lon_apply(control, coarse_lon, fine_lon), time_factor), lat_factor)
    total_weight = jnp.sum(area_weight)
    hourly = jnp.sum(increment, axis=(1, 2))
    flux_field = prior_flux + increment - area_weight[None] * (hourly / total_weight)[:, None, None]
    flux_rows = flux_field.astype(jnp.bfloat16).reshape(-1, footprint_weights.shape[2])
    tile_count = flux_rows.shape[0] // control.shape[0]
    row_index = (footprint_hours * tile_count + footprint_tiles).astype(jnp.int32)
    picked = flux_rows[row_index].astype(jnp.float32)
    weights_wide = footprint_weights.astype(jnp.float32)
    predicted = jnp.einsum('skc,skc->s', picked, weights_wide)
    misfit = (predicted - observations) / error_variance
    contrib = weights_wide * misfit[:, None, None]
    grad_rows = jnp.zeros(flux_rows.shape, jnp.float32).at[row_index.reshape(-1)].add(contrib.reshape(-1, flux_rows.shape[1]))
    grad_flux = grad_rows.reshape(prior_flux.shape)
    weighted = jnp.sum(area_weight[None] * grad_flux, axis=(1, 2))
    projected = grad_flux - (weighted / total_weight)[:, None, None]
    back = lon_adjoint(time_adjoint(lat_adjoint(projected, lat_factor), time_factor), coarse_lon, fine_lon)
    return control + back, misfit
```

```python
import functools

import jax
import jax.numpy as jnp
from jax import lax
from jax.experimental import pallas as pl
from jax.experimental.pallas import tpu as pltpu
from jax.sharding import PartitionSpec as P

highest = lax.Precision.HIGHEST


def lon_apply(field, coarse_lon, fine_lon):
    shaped = field.reshape(field.shape[0], field.shape[1], coarse_lon.shape[0], fine_lon.shape[0])
    shaped = jnp.einsum("hapq,fq->hapf", shaped, fine_lon, precision=highest)
    shaped = jnp.einsum("hapf,cp->hacf", shaped, coarse_lon, precision=highest)
    return shaped.reshape(field.shape)


def lon_adjoint(field, coarse_lon, fine_lon):
    shaped = field.reshape(field.shape[0], field.shape[1], coarse_lon.shape[0], fine_lon.shape[0])
    shaped = jnp.einsum("hapq,qf->hapf", shaped, fine_lon, precision=highest)
    shaped = jnp.einsum("hapf,pc->hacf", shaped, coarse_lon, precision=highest)
    return shaped.reshape(field.shape)


def time_apply(field, time_factor):
    return jnp.einsum("gh,hab->gab", time_factor, field, precision=highest)


def time_adjoint(field, time_factor):
    return jnp.einsum("hg,hab->gab", time_factor, field, precision=highest)


def lat_apply(field, lat_factor):
    return jnp.einsum("ca,hab->hcb", lat_factor, field, precision=highest)


def lat_adjoint(field, lat_factor):
    return jnp.einsum("ac,hab->hcb", lat_factor, field, precision=highest)


def to_columns(field):
    return lax.all_to_all(field, "cells", split_axis=2, concat_axis=1, tiled=True)


def to_rows(field):
    return lax.all_to_all(field, "cells", split_axis=1, concat_axis=2, tiled=True)


def by_latitude(
    control,
    prior_flux,
    area_weight,
    time_factor,
    lat_factor,
    coarse_lon,
    fine_lon,
    footprint_tiles,
    footprint_hours,
    footprint_weights,
    observations,
    error_variance,
):
    devices = lax.axis_size("cells")
    hours_count = control.shape[0]
    tile_width = footprint_weights.shape[2]
    spread = lon_apply(control, coarse_lon, fine_lon)
    spread = time_apply(spread, time_factor)
    increment = to_rows(lat_apply(to_columns(spread), lat_factor))
    hourly, total_weight = lax.psum(
        (jnp.sum(increment, axis=(1, 2)), jnp.sum(area_weight)), "cells"
    )
    flux_field = prior_flux + increment - area_weight[None] * (hourly / total_weight)[:, None, None]
    flux_rows = flux_field.astype(jnp.bfloat16).reshape(-1, tile_width)
    tile_count = flux_rows.shape[0] // hours_count
    slot_total = footprint_tiles.size
    capacity = 2 * slot_total // devices
    owners = (footprint_tiles // tile_count).reshape(-1)
    row_index = (footprint_hours * tile_count + footprint_tiles % tile_count).reshape(-1)
    order = jnp.argsort(owners, stable=True)
    sorted_owners = owners[order]
    starts = jnp.searchsorted(sorted_owners, jnp.arange(devices, dtype=jnp.int32))
    ranked = jnp.arange(slot_total, dtype=jnp.int32) - starts[sorted_owners]
    target = jnp.zeros((slot_total,), jnp.int32).at[order].set(sorted_owners * capacity + ranked)
    weights_flat = footprint_weights.reshape(slot_total, tile_width)
    request_rows = (
        jnp.zeros((devices * capacity,), jnp.int32)
        .at[target]
        .set(row_index)
        .reshape(devices, capacity)
    )
    send_weights = (
        jnp.zeros((devices * capacity, tile_width), jnp.bfloat16).at[target].set(weights_flat)
    )
    got_weights, got_rows = (
        lax.all_to_all(
            send_weights.reshape(devices, capacity, tile_width),
            "cells",
            split_axis=0,
            concat_axis=0,
            tiled=True,
        ),
        lax.all_to_all(request_rows, "cells", split_axis=0, concat_axis=0, tiled=True),
    )
    got_index = got_rows.reshape(-1)
    got_flat = got_weights.reshape(-1, tile_width)
    shares = jnp.einsum(
        "sc,sc->s", flux_rows[got_index], got_flat, preferred_element_type=jnp.float32
    )
    returned = lax.all_to_all(
        shares.reshape(devices, capacity), "cells", split_axis=0, concat_axis=0, tiled=True
    )
    predicted = returned.reshape(-1)[target].reshape(footprint_tiles.shape).sum(axis=1)
    misfit = (predicted - observations) / error_variance
    slot_misfit = jnp.broadcast_to(misfit[:, None], footprint_tiles.shape).reshape(-1)
    send_misfit = jnp.zeros((devices * capacity,), jnp.float32).at[target].set(slot_misfit)
    got_misfit = lax.all_to_all(
        send_misfit.reshape(devices, capacity), "cells", split_axis=0, concat_axis=0, tiled=True
    )
    contrib = got_flat * got_misfit.reshape(-1)[:, None]
    grad_rows = jnp.zeros(flux_rows.shape, jnp.float32).at[got_index].add(contrib)
    grad_flux = grad_rows.reshape(prior_flux.shape)
    weighted = lax.psum(jnp.sum(area_weight[None] * grad_flux, axis=(1, 2)), "cells")
    projected = grad_flux - (weighted / total_weight)[:, None, None]
    back = to_rows(lat_adjoint(to_columns(projected), lat_factor))
    back = time_adjoint(back, time_factor)
    back = lon_adjoint(back, coarse_lon, fine_lon)
    return (control + back, misfit)


MESH_BUDGET = 56 * 1024 * 1024
LANES = 128
SUB = 8


def dot(left, right, left_dim, right_dim):
    return lax.dot_general(
        left,
        right,
        (((left_dim,), (right_dim,)), ((), ())),
        precision=highest,
        preferred_element_type=jnp.float32,
    )


def iota(shape, dim):
    return lax.broadcasted_iota(jnp.int32, shape, dim)


def spread_matrix(factor, repeat, adjoint):
    size = factor.shape[0]
    pick = (iota((size * repeat, size), 0) // repeat == iota((size * repeat, size), 1)).astype(jnp.float32)
    wide = dot(dot(pick, factor, 1, 1 if adjoint else 0), pick, 1, 1)
    whole = (size * repeat, size * repeat)
    return jnp.where(iota(whole, 0) % repeat == iota(whole, 1) % repeat, wide, 0.0)


def encode(blocks, scales, at, out_ref, column):
    largest = jnp.maximum(jnp.max(jnp.abs(blocks), axis=(1, 2), keepdims=True), 1e-33)
    out_ref[:, at, :] = jnp.round(blocks * (32767.0 / largest)).astype(jnp.int32).astype(jnp.int16)
    return jnp.where(iota(scales.shape, 2) == column, largest * (1.0 / 32767.0), scales)


def decode(coded, steps, chunk):
    rows = coded.shape[0]
    pick = (iota((rows, LANES), 1) == iota((rows, LANES), 0) // chunk).astype(jnp.float32)
    return coded.astype(jnp.int32).astype(jnp.float32) * dot(pick, jnp.broadcast_to(steps, (LANES, LANES)), 1, 1)


def split(value, size):
    if size & (size - 1) == 0:
        return lax.shift_right_logical(value, size.bit_length() - 1), value & (size - 1)
    return lax.div(value, size), lax.rem(value, size)


def greet(devices, me):
    barrier = pltpu.get_barrier_semaphore()
    for step in range(1, devices):
        pl.semaphore_signal(
            barrier, inc=1, device_id={"cells": lax.rem(me + step, devices)}, device_id_type=pl.DeviceIdType.MESH
        )
    pl.semaphore_wait(barrier, devices - 1)


def send_to(devices, me, step, source, target, send_sem, recv_sem):
    return pltpu.make_async_remote_copy(
        src_ref=source,
        dst_ref=target,
        send_sem=send_sem,
        recv_sem=recv_sem,
        device_id={"cells": lax.rem(me + step, devices)},
        device_id_type=pl.DeviceIdType.MESH,
    )


def forward_kernel(
    devices, x_ref, area_ref, time_ref, lat_ref, coarse_ref, fine_ref,
    inc_ref, area_out, totals_ref,
    work, sums, sendb, recvb, small_out, small_in, send_sem, recv_sem, small_send, small_recv,
):
    me = lax.axis_index("cells")
    rows = x_ref.shape[0]
    hours = time_ref.shape[0]
    chunk = rows // devices
    time_wide = spread_matrix(time_ref[...], SUB, False)
    coarse_wide = spread_matrix(coarse_ref[...], chunk, False)

    def fine_step(p, carry):
        part = x_ref[:, pl.ds(pl.multiple_of(p * LANES, LANES), LANES)]
        work[p] = dot(dot(time_wide, part, 1, 0), fine_ref[...], 1, 1)
        return carry

    lax.fori_loop(0, devices, fine_step, 0)

    def coarse_step(r, carry):
        at = pl.ds(pl.multiple_of(r * chunk, chunk), chunk)
        mixed = dot(coarse_wide, work[:, at, :].reshape(devices * chunk, LANES), 1, 0).reshape(devices, chunk, LANES)
        sums[at, :] = jnp.sum(mixed, axis=0)
        return encode(mixed, carry, at, sendb, r)

    scales = lax.fori_loop(0, devices, coarse_step, jnp.zeros((devices, SUB, LANES), jnp.float32))
    greet(devices, me)
    copies = []
    for step in range(1, devices):
        peer = lax.rem(me + step, devices)
        copies.append(send_to(devices, me, step, sendb.at[peer], recvb.at[me], send_sem.at[step], recv_sem.at[step]))
        copies[-1].start()

    ones = jnp.ones((SUB, LANES), jnp.float32)
    lat_sums = dot(ones, lat_ref[...], 1, 0)
    place = (iota((LANES, rows), 0) == SUB * me + iota((LANES, rows), 1) % SUB).astype(jnp.float32)
    lat_row = dot(lat_sums, place, 1, 0)[0:1]
    hour_weights = jnp.where(iota((LANES, rows), 0) == iota((LANES, rows), 1) // SUB, lat_row, 0.0)
    mine = dot(ones, dot(hour_weights, sums[...], 1, 0), 1, 1)
    area_total = jnp.sum(jnp.sum(area_ref[...], axis=1, keepdims=True), axis=0, keepdims=True)
    mine = jnp.where(iota((SUB, LANES), 1) == hours, area_total, mine)
    for p in range(devices):
        small_out[p, 0:SUB] = area_ref[:, p * LANES:(p + 1) * LANES]
        small_out[p, SUB:2 * SUB] = jnp.where(iota((SUB, LANES), 0) < SUB // 2, mine, scales[p])
    for step in range(1, devices):
        peer = lax.rem(me + step, devices)
        copies.append(
            send_to(devices, me, step, small_out.at[peer], small_in.at[me], small_send.at[step], small_recv.at[step])
        )
        copies[-1].start()
    recvb[me] = sendb[me]
    small_in[me] = small_out[me]
    for copy in copies:
        copy.wait()
    total = small_in[0, SUB:SUB + 1]
    for p in range(1, devices):
        total = total + small_in[p, SUB:SUB + 1]
    total = jnp.broadcast_to(total, (SUB, LANES))
    weight = total[:, hours:hours + 1]
    totals_ref[...] = jnp.where(iota((SUB, LANES), 1) == hours, total, total / weight)
    for p in range(devices):
        area_out[SUB * p:SUB * (p + 1), :] = small_in[p, 0:SUB]
        work[p] = decode(recvb[p], small_in[p, 2 * SUB - 1:2 * SUB], chunk)
    lat = lat_ref[...]

    def lat_step(h, carry):
        at = pl.ds(pl.multiple_of(h * SUB, SUB), SUB)
        column = work[:, at, :].reshape(devices * SUB, LANES)
        inc_ref[pl.ds(pl.multiple_of(h * LANES, LANES), LANES), :] = dot(lat, column, 1, 0)
        return carry

    lax.fori_loop(0, hours, lat_step, 0, unroll=4)


def share_kernel(
    devices, slots, foot, lists, mean, weights_ref, inc_ref, prior_ref, area_ref, out_ref, wide, prior_rows, shares
):
    me = lax.axis_index("cells")
    rows = prior_ref.shape[0]
    soundings = slots // foot
    stride = lists.shape[0] // (2 * devices)

    def widen(s, carry):
        at = pl.ds(pl.multiple_of(s * slots, slots), slots)
        wide[at, :] = weights_ref[s].astype(jnp.float32)
        shares[at, :] = jnp.zeros((slots, LANES), jnp.float32)
        return carry

    lax.fori_loop(0, devices, widen, 0)

    def prior_step(h, carry):
        level = mean[h]
        for p in range(devices):
            lanes = slice(p * LANES, (p + 1) * LANES)
            prior_rows[pl.ds(pl.multiple_of(p * rows + h * SUB, SUB), SUB), :] = (
                prior_ref[pl.ds(pl.multiple_of(h * SUB, SUB), SUB), lanes] - area_ref[:, lanes] * level
            )
        return carry

    lax.fori_loop(0, rows // SUB, prior_step, 0)

    def each_source(which, table, add):
        def source(s, carry):
            base = (2 * s + which) * stride
            low = lists[base + slots + me]
            high = lists[base + slots + me + 1]

            def group(first, count):
                products, places = [], []
                for j in range(count):
                    value = lists[base + first + j]
                    row, slot = split(value, slots)
                    row = split(row, table.shape[0])[1]
                    sounding, k = split(slot, foot)
                    place = k * (devices * soundings) + s * soundings + sounding
                    product = table[pl.ds(row, 1), :] * wide[pl.ds(s * slots + slot, 1), :]
                    if add:
                        product = product + shares[pl.ds(place, 1), :]
                    products.append(product)
                    places.append(place)
                for place, product in zip(places, products):
                    shares[pl.ds(place, 1), :] = product

            groups = (high - low) // 8

            def full(i, inner):
                group(low + i * 8, 8)
                return inner

            def rest(i, inner):
                group(i, 1)
                return inner

            lax.fori_loop(0, groups, full, 0)
            lax.fori_loop(low + groups * 8, high, rest, 0)
            return carry

        lax.fori_loop(0, devices, source, 0)

    each_source(0, inc_ref, False)
    each_source(1, prior_rows, True)
    ones = jnp.ones((SUB, LANES), jnp.float32)

    def collect(s, carry):
        summed = shares[pl.ds(pl.multiple_of(s * soundings, soundings), soundings), :]
        for k in range(1, foot):
            at = pl.multiple_of(k * devices * soundings + s * soundings, soundings)
            summed = summed + shares[pl.ds(at, soundings), :]
        out_ref[s] = dot(ones, summed, 1, 1)
        return carry

    lax.fori_loop(0, devices, collect, 0)


def misfit_kernel(
    devices, part_ref, seen_ref, variance_ref, all_ref, own_ref,
    got, spread, mine, send_sem, recv_sem, back_send, back_recv,
):
    me = lax.axis_index("cells")
    greet(devices, me)
    copies = []
    for step in range(1, devices):
        peer = lax.rem(me + step, devices)
        copies.append(send_to(devices, me, step, part_ref.at[peer], got.at[me], send_sem.at[step], recv_sem.at[step]))
        copies[-1].start()
    got[me] = part_ref[me]
    for copy in copies:
        copy.wait()
    predicted = got[0]
    for p in range(1, devices):
        predicted = predicted + got[p]
    misfit = (predicted - seen_ref[...]) / variance_ref[...]
    mine[...] = misfit
    copies = []
    for step in range(1, devices):
        copies.append(send_to(devices, me, step, mine, spread.at[me], back_send.at[step], back_recv.at[step]))
        copies[-1].start()
    spread[me] = misfit
    own_ref[...] = misfit
    for copy in copies:
        copy.wait()
    all_ref[...] = spread[...]


def scatter_kernel(devices, slots, foot, lists, misfit, weights_ref, grad_ref, wide):
    me = lax.axis_index("cells")
    soundings = slots // foot
    stride = lists.shape[0] // (2 * devices)
    cells = grad_ref.shape[0]

    def widen(s, carry):
        at = pl.ds(pl.multiple_of(s * slots, slots), slots)
        wide[at, :] = weights_ref[s].astype(jnp.float32)
        part = cells // devices
        grad_ref[pl.ds(pl.multiple_of(s * part, part), part), :] = jnp.zeros((part, LANES), jnp.float32)
        return carry

    lax.fori_loop(0, devices, widen, 0)

    def source(s, carry):
        base = 2 * s * stride
        low = lists[base + slots + me]
        high = lists[base + slots + me + 1]

        def group(first, count):
            products, places = [], []
            for j in range(count):
                value = lists[base + first + j]
                row, slot = split(value, slots)
                places.append(split(row, cells)[1])
                products.append(wide[pl.ds(s * slots + slot, 1), :] * misfit[s * soundings + split(slot, foot)[0]])
            for place, product in zip(places, products):
                grad_ref[pl.ds(place, 1), :] += product

        groups = (high - low) // 8

        def full(i, inner):
            group(low + i * 8, 8)
            return inner

        def rest(i, inner):
            group(i, 1)
            return inner

        lax.fori_loop(0, groups, full, 0)
        lax.fori_loop(low + groups * 8, high, rest, 0)
        return carry

    lax.fori_loop(0, devices, source, 0)


def adjoint_kernel(
    devices, grad_ref, area_ref, totals_ref, x_ref, time_ref, lat_ref, coarse_ref, fine_ref, out_ref,
    work, mixed, hour_sums, sendb, recvb, small_out, small_in, send_sem, recv_sem, small_send, small_recv,
):
    me = lax.axis_index("cells")
    rows = x_ref.shape[0]
    hours = time_ref.shape[0]
    chunk = rows // devices
    lat = lat_ref[...].T
    hour_sums[...] = jnp.zeros(hour_sums.shape, jnp.float32)

    def lat_step(h, carry):
        field = grad_ref[pl.ds(pl.multiple_of(h * LANES, LANES), LANES), :]
        at = pl.ds(pl.multiple_of(h * SUB, SUB), SUB)
        work[:, at, :] = dot(lat, field, 1, 0).reshape(devices, SUB, LANES)
        hour_sums[pl.ds(h, 1), :] = jnp.sum(field * area_ref[...], axis=0, keepdims=True)
        return carry

    lax.fori_loop(0, hours, lat_step, 0, unroll=4)

    def encode_step(r, carry):
        at = pl.ds(pl.multiple_of(r * chunk, chunk), chunk)
        return encode(work[:, at, :], carry, at, sendb, r)

    scales = lax.fori_loop(0, devices, encode_step, jnp.zeros((devices, SUB, LANES), jnp.float32))
    greet(devices, me)
    copies = []
    for step in range(1, devices):
        peer = lax.rem(me + step, devices)
        copies.append(send_to(devices, me, step, sendb.at[peer], recvb.at[me], send_sem.at[step], recv_sem.at[step]))
        copies[-1].start()
    ones = jnp.ones((SUB, LANES), jnp.float32)
    weighted = dot(ones, hour_sums[...], 1, 1)
    for p in range(devices):
        small_out[p] = jnp.where(iota((SUB, LANES), 0) < SUB // 2, weighted, scales[p])
    for step in range(1, devices):
        peer = lax.rem(me + step, devices)
        copies.append(
            send_to(devices, me, step, small_out.at[peer], small_in.at[me], small_send.at[step], small_recv.at[step])
        )
        copies[-1].start()
    small_in[me] = small_out[me]
    recvb[me] = sendb[me]
    time_wide = spread_matrix(time_ref[...], SUB, True)
    coarse_wide = spread_matrix(coarse_ref[...], chunk, True)
    square = jnp.ones((LANES, LANES), jnp.float32)
    lat_sums = dot(square, lat_ref[...], 1, 0)
    place = (iota((rows, LANES), 1) == SUB * me + iota((rows, LANES), 0) % SUB).astype(jnp.float32)
    lat_column = dot(place, lat_sums, 1, 1)
    for copy in copies:
        copy.wait()
    total = small_in[0, 0:1]
    for p in range(1, devices):
        total = total + small_in[p, 0:1]
    level = total / totals_ref[0:1, hours:hours + 1]
    hour_of = (iota((rows, LANES), 1) == iota((rows, LANES), 0) // SUB).astype(jnp.float32)
    level_column = dot(hour_of, jnp.broadcast_to(level, (LANES, LANES)), 1, 1)
    shift = lat_column * level_column
    for p in range(devices):
        work[p] = decode(recvb[p], small_in[p, SUB - 1:SUB], chunk) - shift

    def coarse_step(r, carry):
        at = pl.ds(pl.multiple_of(r * chunk, chunk), chunk)
        mixed[:, at, :] = dot(coarse_wide, work[:, at, :].reshape(devices * chunk, LANES), 1, 0).reshape(
            devices, chunk, LANES
        )
        return carry

    lax.fori_loop(0, devices, coarse_step, 0)

    def fine_step(p, carry):
        lanes = pl.ds(pl.multiple_of(p * LANES, LANES), LANES)
        out_ref[:, lanes] = x_ref[:, lanes] + dot(time_wide, dot(mixed[p], fine_ref[...], 1, 0), 1, 0)
        return carry

    lax.fori_loop(0, devices, fine_step, 0)


def f32(*shape):
    return jax.ShapeDtypeStruct(shape, jnp.float32)


def vmem(count):
    return [pl.BlockSpec(memory_space=pltpu.VMEM)] * count


def smem(count):
    return [pl.BlockSpec(memory_space=pltpu.SMEM)] * count


def by_longitude(
    control,
    prior_flux,
    area_weight,
    time_factor,
    lat_factor,
    coarse_lon,
    fine_lon,
    footprint_tiles,
    footprint_hours,
    footprint_weights,
    observations,
    error_variance,
):
    devices = lax.axis_size("cells")
    hours, lat_rows, longitude = control.shape
    latitude = lat_factor.shape[0]
    rows = hours * lat_rows
    foot = footprint_tiles.shape[1]
    slots = footprint_tiles.size
    soundings = footprint_tiles.shape[0]
    cells = hours * latitude

    gathered = lax.all_gather(footprint_weights.reshape(slots, LANES), "cells", axis=0, tiled=False)
    tiles = footprint_tiles.reshape(-1)
    hour = footprint_hours.reshape(-1)
    lat = tiles // devices
    tile = tiles % devices
    slot = jnp.arange(slots, dtype=jnp.int32)
    by_lon = (tile * cells + hour * latitude + lat) * slots + slot
    by_lat = ((lat // lat_rows) * cells + tile * rows + hour * lat_rows + lat % lat_rows) * slots + slot
    ordered = lax.sort(jnp.stack([by_lon, by_lat]), dimension=1)
    edges = jnp.arange(LANES, dtype=jnp.int32) * (cells * slots)
    starts = jnp.sum((ordered[:, None, :] < edges[None, :, None]).astype(jnp.int32), axis=2)
    lists = lax.all_gather(jnp.concatenate([ordered, starts], axis=1).reshape(-1), "cells", axis=0, tiled=True)

    x = control.reshape(rows, longitude)
    prior = prior_flux.reshape(rows, longitude)
    sems = [pltpu.SemaphoreType.DMA((devices,))] * 4
    blocks = (devices, rows, LANES)
    limits = dict(vmem_limit_bytes=MESH_BUDGET, has_side_effects=True)
    increment, area_column, totals = pl.pallas_call(
        functools.partial(forward_kernel, devices),
        out_shape=(f32(cells, LANES), f32(latitude, LANES), f32(SUB, LANES)),
        in_specs=vmem(6),
        out_specs=tuple(vmem(3)),
        scratch_shapes=[
            pltpu.VMEM(blocks, jnp.float32),
            pltpu.VMEM((rows, LANES), jnp.float32),
            pltpu.VMEM(blocks, jnp.int16),
            pltpu.VMEM(blocks, jnp.int16),
            pltpu.VMEM((devices, 2 * SUB, LANES), jnp.float32),
            pltpu.VMEM((devices, 2 * SUB, LANES), jnp.float32),
        ] + sems,
        compiler_params=pltpu.CompilerParams(collective_id=0, **limits),
    )(x, area_weight, time_factor, lat_factor, coarse_lon, fine_lon)

    partial = pl.pallas_call(
        functools.partial(share_kernel, devices, slots, foot),
        out_shape=f32(devices, SUB, soundings),
        in_specs=smem(2) + vmem(4),
        out_specs=vmem(1)[0],
        scratch_shapes=[
            pltpu.VMEM((devices * slots, LANES), jnp.float32),
            pltpu.VMEM((cells, LANES), jnp.float32),
            pltpu.VMEM((devices * slots, LANES), jnp.float32),
        ],
        compiler_params=pltpu.CompilerParams(vmem_limit_bytes=MESH_BUDGET),
    )(lists, totals[0], gathered, increment, prior, area_weight)

    small = pltpu.VMEM((devices, SUB, LANES), jnp.float32)
    every, own = pl.pallas_call(
        functools.partial(misfit_kernel, devices),
        out_shape=(f32(devices, SUB, soundings), f32(SUB, soundings)),
        in_specs=vmem(3),
        out_specs=tuple(vmem(2)),
        scratch_shapes=[small, small, pltpu.VMEM((SUB, LANES), jnp.float32)] + sems,
        compiler_params=pltpu.CompilerParams(collective_id=1, **limits),
    )(partial, observations.reshape(1, soundings), error_variance.reshape(1, soundings))

    grad = pl.pallas_call(
        functools.partial(scatter_kernel, devices, slots, foot),
        out_shape=f32(cells, LANES),
        in_specs=smem(2) + vmem(1),
        out_specs=vmem(1)[0],
        scratch_shapes=[pltpu.VMEM((devices * slots, LANES), jnp.float32)],
        compiler_params=pltpu.CompilerParams(vmem_limit_bytes=MESH_BUDGET),
    )(lists, every[:, 0].reshape(-1), gathered)

    gradient = pl.pallas_call(
        functools.partial(adjoint_kernel, devices),
        out_shape=f32(rows, longitude),
        in_specs=vmem(8),
        out_specs=vmem(1)[0],
        scratch_shapes=[
            pltpu.VMEM(blocks, jnp.float32),
            pltpu.VMEM(blocks, jnp.float32),
            pltpu.VMEM((LANES, LANES), jnp.float32),
            pltpu.VMEM(blocks, jnp.int16),
            pltpu.VMEM(blocks, jnp.int16),
            small,
            small,
        ] + sems,
        compiler_params=pltpu.CompilerParams(collective_id=2, **limits),
    )(grad, area_column, totals, x, time_factor, lat_factor, coarse_lon, fine_lon)
    return gradient.reshape(control.shape), own[0]


def fits(devices, control, coarse_lon, fine_lon, lat_factor, footprint_tiles):
    return (
        devices == coarse_lon.shape[0]
        and fine_lon.shape[0] == LANES
        and control.shape[1] == SUB
        and lat_factor.shape[0] == LANES
        and footprint_tiles.shape[0] == LANES
        and (control.shape[0] * SUB) % (16 * devices) == 0
        and control.shape[0] < LANES
        and devices * control.shape[0] * LANES * footprint_tiles.size < 2**31
        and devices < LANES
    )


def per_device(*arrays):
    devices = lax.axis_size("cells")
    control, lat_factor, coarse_lon, fine_lon, footprint_tiles = (arrays[i] for i in (0, 4, 5, 6, 7))
    if fits(devices, control, coarse_lon, fine_lon, lat_factor, footprint_tiles):
        return by_longitude(*arrays)
    return by_latitude(*arrays)


def solution(mesh):
    placed = (
        P("ens", "cells", None),
        P(None, "cells", None),
        P("cells", None),
        P(),
        P(),
        P(),
        P(),
        P("cells", None),
        P("cells", None),
        P("cells", None, None),
        P(("ens", "cells")),
        P("cells"),
    )
    return jax.shard_map(
        per_device,
        mesh=mesh,
        in_specs=placed,
        out_specs=(P("ens", "cells", None), P(("ens", "cells"))),
        check_vma=False,
    )
```

```python
import functools

import jax
import jax.numpy as jnp
from jax import lax
from jax.experimental import pallas as pl
from jax.experimental.pallas import tpu as pltpu
from jax.sharding import PartitionSpec as P

highest = lax.Precision.HIGHEST


def lon_apply(field, coarse_lon, fine_lon):
    shaped = field.reshape(field.shape[0], field.shape[1], coarse_lon.shape[0], fine_lon.shape[0])
    shaped = jnp.einsum("hapq,fq->hapf", shaped, fine_lon, precision=highest)
    shaped = jnp.einsum("hapf,cp->hacf", shaped, coarse_lon, precision=highest)
    return shaped.reshape(field.shape)


def lon_adjoint(field, coarse_lon, fine_lon):
    shaped = field.reshape(field.shape[0], field.shape[1], coarse_lon.shape[0], fine_lon.shape[0])
    shaped = jnp.einsum("hapq,qf->hapf", shaped, fine_lon, precision=highest)
    shaped = jnp.einsum("hapf,pc->hacf", shaped, coarse_lon, precision=highest)
    return shaped.reshape(field.shape)


def time_apply(field, time_factor):
    return jnp.einsum("gh,hab->gab", time_factor, field, precision=highest)


def time_adjoint(field, time_factor):
    return jnp.einsum("hg,hab->gab", time_factor, field, precision=highest)


def lat_apply(field, lat_factor):
    return jnp.einsum("ca,hab->hcb", lat_factor, field, precision=highest)


def lat_adjoint(field, lat_factor):
    return jnp.einsum("ac,hab->hcb", lat_factor, field, precision=highest)


def to_columns(field):
    return lax.all_to_all(field, "cells", split_axis=2, concat_axis=1, tiled=True)


def to_rows(field):
    return lax.all_to_all(field, "cells", split_axis=1, concat_axis=2, tiled=True)


def by_latitude(
    control,
    prior_flux,
    area_weight,
    time_factor,
    lat_factor,
    coarse_lon,
    fine_lon,
    footprint_tiles,
    footprint_hours,
    footprint_weights,
    observations,
    error_variance,
):
    devices = lax.axis_size("cells")
    hours_count = control.shape[0]
    tile_width = footprint_weights.shape[2]
    spread = lon_apply(control, coarse_lon, fine_lon)
    spread = time_apply(spread, time_factor)
    increment = to_rows(lat_apply(to_columns(spread), lat_factor))
    hourly, total_weight = lax.psum(
        (jnp.sum(increment, axis=(1, 2)), jnp.sum(area_weight)), "cells"
    )
    flux_field = prior_flux + increment - area_weight[None] * (hourly / total_weight)[:, None, None]
    flux_rows = flux_field.astype(jnp.bfloat16).reshape(-1, tile_width)
    tile_count = flux_rows.shape[0] // hours_count
    slot_total = footprint_tiles.size
    capacity = 2 * slot_total // devices
    owners = (footprint_tiles // tile_count).reshape(-1)
    row_index = (footprint_hours * tile_count + footprint_tiles % tile_count).reshape(-1)
    order = jnp.argsort(owners, stable=True)
    sorted_owners = owners[order]
    starts = jnp.searchsorted(sorted_owners, jnp.arange(devices, dtype=jnp.int32))
    ranked = jnp.arange(slot_total, dtype=jnp.int32) - starts[sorted_owners]
    target = jnp.zeros((slot_total,), jnp.int32).at[order].set(sorted_owners * capacity + ranked)
    weights_flat = footprint_weights.reshape(slot_total, tile_width)
    request_rows = (
        jnp.zeros((devices * capacity,), jnp.int32)
        .at[target]
        .set(row_index)
        .reshape(devices, capacity)
    )
    send_weights = (
        jnp.zeros((devices * capacity, tile_width), jnp.bfloat16).at[target].set(weights_flat)
    )
    got_weights, got_rows = (
        lax.all_to_all(
            send_weights.reshape(devices, capacity, tile_width),
            "cells",
            split_axis=0,
            concat_axis=0,
            tiled=True,
        ),
        lax.all_to_all(request_rows, "cells", split_axis=0, concat_axis=0, tiled=True),
    )
    got_index = got_rows.reshape(-1)
    got_flat = got_weights.reshape(-1, tile_width)
    shares = jnp.einsum(
        "sc,sc->s", flux_rows[got_index], got_flat, preferred_element_type=jnp.float32
    )
    returned = lax.all_to_all(
        shares.reshape(devices, capacity), "cells", split_axis=0, concat_axis=0, tiled=True
    )
    predicted = returned.reshape(-1)[target].reshape(footprint_tiles.shape).sum(axis=1)
    misfit = (predicted - observations) / error_variance
    slot_misfit = jnp.broadcast_to(misfit[:, None], footprint_tiles.shape).reshape(-1)
    send_misfit = jnp.zeros((devices * capacity,), jnp.float32).at[target].set(slot_misfit)
    got_misfit = lax.all_to_all(
        send_misfit.reshape(devices, capacity), "cells", split_axis=0, concat_axis=0, tiled=True
    )
    contrib = got_flat * got_misfit.reshape(-1)[:, None]
    grad_rows = jnp.zeros(flux_rows.shape, jnp.float32).at[got_index].add(contrib)
    grad_flux = grad_rows.reshape(prior_flux.shape)
    weighted = lax.psum(jnp.sum(area_weight[None] * grad_flux, axis=(1, 2)), "cells")
    projected = grad_flux - (weighted / total_weight)[:, None, None]
    back = to_rows(lat_adjoint(to_columns(projected), lat_factor))
    back = time_adjoint(back, time_factor)
    back = lon_adjoint(back, coarse_lon, fine_lon)
    return (control + back, misfit)


MESH_BUDGET = 56 * 1024 * 1024
LANES = 128
SUB = 8


def dot(left, right, left_dim, right_dim):
    return lax.dot_general(
        left,
        right,
        (((left_dim,), (right_dim,)), ((), ())),
        precision=highest,
        preferred_element_type=jnp.float32,
    )


def iota(shape, dim):
    return lax.broadcasted_iota(jnp.int32, shape, dim)


def halves(value):
    high = value.astype(jnp.bfloat16)
    return high, (value - high.astype(jnp.float32)).astype(jnp.bfloat16)


def product(left, right):
    return lax.dot_general(left, right, (((1,), (0,)), ((), ())), preferred_element_type=jnp.float32)


def stacked(value):
    high, low = halves(value)
    above = jnp.concatenate([high, low], axis=1)
    below = jnp.concatenate([high, jnp.zeros_like(high)], axis=1)
    return jnp.concatenate([above, below], axis=0)


def fold(wide):
    return wide[:, :LANES] + wide[:, LANES:]


def left_wide(factor, data):
    high, low = halves(data)
    return fold(product(factor[0], jnp.concatenate([high, low], axis=1))) + product(factor[1], high)


def left_square(factor, data):
    return fold(product(jnp.concatenate(factor, axis=1), stacked(data)))


def right_square(data, factor):
    return fold(product(jnp.concatenate(halves(data), axis=1), factor))


def spread_matrix(factor, repeat, adjoint):
    size = factor.shape[0]
    pick = (iota((size * repeat, size), 0) // repeat == iota((size * repeat, size), 1)).astype(jnp.float32)
    wide = dot(dot(pick, factor, 1, 1 if adjoint else 0), pick, 1, 1)
    whole = (size * repeat, size * repeat)
    return jnp.where(iota(whole, 0) % repeat == iota(whole, 1) % repeat, wide, 0.0)


def encode(blocks, scales, at, out_ref, column):
    largest = jnp.maximum(jnp.max(jnp.abs(blocks), axis=(1, 2), keepdims=True), 1e-33)
    out_ref[:, at, :] = jnp.round(blocks * (32767.0 / largest)).astype(jnp.int32).astype(jnp.int16)
    return jnp.where(iota(scales.shape, 2) == column, largest * (1.0 / 32767.0), scales)


def decode(coded, steps, chunk):
    rows = coded.shape[0]
    pick = (iota((rows, LANES), 1) == iota((rows, LANES), 0) // chunk).astype(jnp.float32)
    return coded.astype(jnp.int32).astype(jnp.float32) * dot(pick, jnp.broadcast_to(steps, (LANES, LANES)), 1, 1)


def split(value, size):
    if size & (size - 1) == 0:
        return lax.shift_right_logical(value, size.bit_length() - 1), value & (size - 1)
    return lax.div(value, size), lax.rem(value, size)


def greet(devices, me):
    barrier = pltpu.get_barrier_semaphore()
    for step in range(1, devices):
        pl.semaphore_signal(
            barrier, inc=1, device_id={"cells": lax.rem(me + step, devices)}, device_id_type=pl.DeviceIdType.MESH
        )
    pl.semaphore_wait(barrier, devices - 1)


def send_to(devices, me, step, source, target, send_sem, recv_sem):
    return pltpu.make_async_remote_copy(
        src_ref=source,
        dst_ref=target,
        send_sem=send_sem,
        recv_sem=recv_sem,
        device_id={"cells": lax.rem(me + step, devices)},
        device_id_type=pl.DeviceIdType.MESH,
    )


class Travel:
    def __init__(self, devices, me, own, everyone, send_sem, recv_sem):
        self.devices, self.me, self.own, self.everyone = devices, me, own, everyone
        self.send_sem, self.recv_sem = send_sem, recv_sem
        self.steps = devices // 4
        self.across = self.across_of(me)
        self.core = me + 1 - 2 * lax.rem(me, 2)
        self.copies = {}

    def across_of(self, device):
        return device + 2 - 4 * lax.rem(lax.div(device, 2), 2)

    def behind(self, device, step):
        return lax.rem(device - 4 * step + self.devices, self.devices)

    def send(self, at, block, peer):
        source = self.own if block is None else self.everyone.at[block]
        copy = pltpu.make_async_remote_copy(
            src_ref=source,
            dst_ref=self.everyone.at[self.me if block is None else block],
            send_sem=self.send_sem.at[at],
            recv_sem=self.recv_sem.at[at],
            device_id={"cells": peer},
            device_id_type=pl.DeviceIdType.MESH,
        )
        copy.start()
        self.copies[at] = copy

    def start(self):
        steps = self.steps
        for step in range(1, steps):
            self.send(step, None, lax.rem(self.me + 4 * step, self.devices))
        self.send(steps, None, self.across)
        self.send(2 * steps, None, self.core)
        self.everyone[self.me] = self.own[...]

    def arrived(self, at, block):
        here = self.everyone.at[block]
        pltpu.make_async_remote_copy(
            src_ref=here,
            dst_ref=here,
            send_sem=self.send_sem.at[at],
            recv_sem=self.recv_sem.at[at],
            device_id={"cells": self.core},
            device_id_type=pl.DeviceIdType.MESH,
        ).wait_recv()

    def first(self):
        for step in range(1, self.steps):
            block = self.behind(self.me, step)
            self.arrived(step, block)
            self.send(self.steps + step, block, self.across)
            self.send(2 * self.steps + step, block, self.core)

    def second(self):
        for step in range(self.steps):
            block = self.behind(self.across, step)
            self.arrived(self.steps + step, block)
            self.send(3 * self.steps + step, block, self.core)

    def finish(self):
        for step in range(self.steps):
            self.arrived(2 * self.steps + step, self.behind(self.core, step))
            self.arrived(3 * self.steps + step, self.behind(self.across_of(self.core), step))
        for copy in self.copies.values():
            copy.wait_send()


def forward_kernel(
    devices, weights_ref, list_ref, x_ref, area_ref, time_ref, lat_ref, coarse_ref, fine_ref,
    inc_ref, area_out, totals_ref, weights_out, list_out,
    work, sums, sendb, recvb, small_out, small_in, list_in, send_sem, recv_sem, small_send, small_recv,
    list_send, list_recv, travel_send, travel_recv,
):
    me = lax.axis_index("cells")
    rows = x_ref.shape[0]
    hours = time_ref.shape[0]
    chunk = rows // devices
    greet(devices, me)
    travel = Travel(devices, me, weights_ref, weights_out, travel_send, travel_recv)
    travel.start()
    copies = []
    for step in range(1, devices):
        copies.append(send_to(devices, me, step, list_ref, list_in.at[me], list_send.at[step], list_recv.at[step]))
        copies[-1].start()
    time_wide = halves(spread_matrix(time_ref[...], SUB, False))
    coarse_wide = halves(spread_matrix(coarse_ref[...], chunk, False))
    fine = stacked(fine_ref[...].T)

    def fine_step(p, carry):
        part = x_ref[:, pl.ds(pl.multiple_of(p * LANES, LANES), LANES)]
        work[p] = right_square(left_wide(time_wide, part), fine)
        return carry

    lax.fori_loop(0, devices, fine_step, 0, unroll=2)
    travel.first()

    def coarse_step(r, carry):
        at = pl.ds(pl.multiple_of(r * chunk, chunk), chunk)
        mixed = left_wide(coarse_wide, work[:, at, :].reshape(devices * chunk, LANES)).reshape(devices, chunk, LANES)
        sums[at, :] = jnp.sum(mixed, axis=0)
        return encode(mixed, carry, at, sendb, r)

    scales = lax.fori_loop(0, devices, coarse_step, jnp.zeros((devices, SUB, LANES), jnp.float32), unroll=2)
    for step in range(1, devices):
        peer = lax.rem(me + step, devices)
        copies.append(send_to(devices, me, step, sendb.at[peer], recvb.at[me], send_sem.at[step], recv_sem.at[step]))
        copies[-1].start()

    ones = jnp.ones((SUB, LANES), jnp.float32)
    lat_sums = dot(ones, lat_ref[...], 1, 0)
    place = (iota((LANES, rows), 0) == SUB * me + iota((LANES, rows), 1) % SUB).astype(jnp.float32)
    lat_row = dot(lat_sums, place, 1, 0)[0:1]
    hour_weights = jnp.where(iota((LANES, rows), 0) == iota((LANES, rows), 1) // SUB, lat_row, 0.0)
    mine = dot(ones, dot(hour_weights, sums[...], 1, 0), 1, 1)
    area_total = jnp.sum(jnp.sum(area_ref[...], axis=1, keepdims=True), axis=0, keepdims=True)
    mine = jnp.where(iota((SUB, LANES), 1) == hours, area_total, mine)
    for p in range(devices):
        small_out[p, 0:SUB] = area_ref[:, p * LANES:(p + 1) * LANES]
        small_out[p, SUB:2 * SUB] = jnp.where(iota((SUB, LANES), 0) < SUB // 2, mine, scales[p])
    for step in range(1, devices):
        peer = lax.rem(me + step, devices)
        copies.append(
            send_to(devices, me, step, small_out.at[peer], small_in.at[me], small_send.at[step], small_recv.at[step])
        )
        copies[-1].start()
    recvb[me] = sendb[me]
    small_in[me] = small_out[me]
    list_in[me] = list_ref[...]
    travel.second()
    for copy in copies:
        copy.wait()
    list_out[...] = list_in[...]
    total = small_in[0, SUB:SUB + 1]
    for p in range(1, devices):
        total = total + small_in[p, SUB:SUB + 1]
    total = jnp.broadcast_to(total, (SUB, LANES))
    weight = total[:, hours:hours + 1]
    totals_ref[...] = jnp.where(iota((SUB, LANES), 1) == hours, total, total / weight)
    for p in range(devices):
        area_out[SUB * p:SUB * (p + 1), :] = small_in[p, 0:SUB]
        work[p] = decode(recvb[p], small_in[p, 2 * SUB - 1:2 * SUB], chunk)
    lat = halves(lat_ref[...])

    def lat_step(h, carry):
        at = pl.ds(pl.multiple_of(h * SUB, SUB), SUB)
        column = work[:, at, :].reshape(devices * SUB, LANES)
        inc_ref[pl.ds(pl.multiple_of(h * LANES, LANES), LANES), :] = left_square(lat, column)
        return carry

    lax.fori_loop(0, hours, lat_step, 0, unroll=4)
    travel.finish()


def share_kernel(
    devices, slots, foot, lists, mean, weights_ref, inc_ref, prior_ref, area_ref, out_ref, wide, prior_rows, shares
):
    me = lax.axis_index("cells")
    rows = prior_ref.shape[0]
    soundings = slots // foot
    stride = lists.shape[0] // (2 * devices)

    def widen(s, carry):
        at = pl.ds(pl.multiple_of(s * slots, slots), slots)
        wide[at, :] = weights_ref[s].astype(jnp.float32)
        shares[at, :] = jnp.zeros((slots, LANES), jnp.float32)
        return carry

    lax.fori_loop(0, devices, widen, 0)

    def prior_step(h, carry):
        level = mean[h]
        for p in range(devices):
            lanes = slice(p * LANES, (p + 1) * LANES)
            prior_rows[pl.ds(pl.multiple_of(p * rows + h * SUB, SUB), SUB), :] = (
                prior_ref[pl.ds(pl.multiple_of(h * SUB, SUB), SUB), lanes] - area_ref[:, lanes] * level
            )
        return carry

    lax.fori_loop(0, rows // SUB, prior_step, 0)

    def each_source(which, table, add):
        def source(s, carry):
            base = (2 * s + which) * stride
            low = lists[base + slots + me]
            high = lists[base + slots + me + 1]

            def group(first, count):
                products, places = [], []
                for j in range(count):
                    value = lists[base + first + j]
                    row, slot = split(value, slots)
                    row = split(row, table.shape[0])[1]
                    sounding, k = split(slot, foot)
                    place = k * (devices * soundings) + s * soundings + sounding
                    product = table[pl.ds(row, 1), :] * wide[pl.ds(s * slots + slot, 1), :]
                    if add:
                        product = product + shares[pl.ds(place, 1), :]
                    products.append(product)
                    places.append(place)
                for place, product in zip(places, products):
                    shares[pl.ds(place, 1), :] = product

            groups = (high - low) // 8

            def full(i, inner):
                group(low + i * 8, 8)
                return inner

            def rest(i, inner):
                group(i, 1)
                return inner

            lax.fori_loop(0, groups, full, 0)
            lax.fori_loop(low + groups * 8, high, rest, 0)
            return carry

        lax.fori_loop(0, devices, source, 0)

    each_source(0, inc_ref, False)
    each_source(1, prior_rows, True)
    ones = jnp.ones((SUB, LANES), jnp.float32)

    def collect(s, carry):
        summed = shares[pl.ds(pl.multiple_of(s * soundings, soundings), soundings), :]
        for k in range(1, foot):
            at = pl.multiple_of(k * devices * soundings + s * soundings, soundings)
            summed = summed + shares[pl.ds(at, soundings), :]
        out_ref[s] = dot(ones, summed, 1, 1)
        return carry

    lax.fori_loop(0, devices, collect, 0)


def misfit_kernel(
    devices, part_ref, seen_ref, variance_ref, all_ref, own_ref,
    got, spread, mine, send_sem, recv_sem, back_send, back_recv,
):
    me = lax.axis_index("cells")
    greet(devices, me)
    copies = []
    for step in range(1, devices):
        peer = lax.rem(me + step, devices)
        copies.append(send_to(devices, me, step, part_ref.at[peer], got.at[me], send_sem.at[step], recv_sem.at[step]))
        copies[-1].start()
    got[me] = part_ref[me]
    for copy in copies:
        copy.wait()
    predicted = got[0]
    for p in range(1, devices):
        predicted = predicted + got[p]
    misfit = (predicted - seen_ref[...]) / variance_ref[...]
    mine[...] = misfit
    copies = []
    for step in range(1, devices):
        copies.append(send_to(devices, me, step, mine, spread.at[me], back_send.at[step], back_recv.at[step]))
        copies[-1].start()
    spread[me] = misfit
    own_ref[...] = misfit
    for copy in copies:
        copy.wait()
    all_ref[...] = spread[...]


def scatter_kernel(devices, slots, foot, lists, misfit, weights_ref, grad_ref, wide):
    me = lax.axis_index("cells")
    soundings = slots // foot
    stride = lists.shape[0] // (2 * devices)
    cells = grad_ref.shape[0]

    def widen(s, carry):
        at = pl.ds(pl.multiple_of(s * slots, slots), slots)
        wide[at, :] = weights_ref[s].astype(jnp.float32)
        part = cells // devices
        grad_ref[pl.ds(pl.multiple_of(s * part, part), part), :] = jnp.zeros((part, LANES), jnp.float32)
        return carry

    lax.fori_loop(0, devices, widen, 0)

    def source(s, carry):
        base = 2 * s * stride
        low = lists[base + slots + me]
        high = lists[base + slots + me + 1]

        def group(first, count):
            products, places = [], []
            for j in range(count):
                value = lists[base + first + j]
                row, slot = split(value, slots)
                places.append(split(row, cells)[1])
                products.append(wide[pl.ds(s * slots + slot, 1), :] * misfit[s * soundings + split(slot, foot)[0]])
            for place, product in zip(places, products):
                grad_ref[pl.ds(place, 1), :] += product

        groups = (high - low) // 8

        def full(i, inner):
            group(low + i * 8, 8)
            return inner

        def rest(i, inner):
            group(i, 1)
            return inner

        lax.fori_loop(0, groups, full, 0)
        lax.fori_loop(low + groups * 8, high, rest, 0)
        return carry

    lax.fori_loop(0, devices, source, 0)


def adjoint_kernel(
    devices, grad_ref, area_ref, totals_ref, x_ref, time_ref, lat_ref, coarse_ref, fine_ref, out_ref,
    work, mixed, hour_sums, sendb, recvb, small_out, small_in, send_sem, recv_sem, small_send, small_recv,
):
    me = lax.axis_index("cells")
    rows = x_ref.shape[0]
    hours = time_ref.shape[0]
    chunk = rows // devices
    lat = halves(lat_ref[...].T)
    hour_sums[...] = jnp.zeros(hour_sums.shape, jnp.float32)

    def lat_step(h, carry):
        field = grad_ref[pl.ds(pl.multiple_of(h * LANES, LANES), LANES), :]
        at = pl.ds(pl.multiple_of(h * SUB, SUB), SUB)
        work[:, at, :] = left_square(lat, field).reshape(devices, SUB, LANES)
        hour_sums[pl.ds(h, 1), :] = jnp.sum(field * area_ref[...], axis=0, keepdims=True)
        return carry

    lax.fori_loop(0, hours, lat_step, 0, unroll=4)

    def encode_step(r, carry):
        at = pl.ds(pl.multiple_of(r * chunk, chunk), chunk)
        return encode(work[:, at, :], carry, at, sendb, r)

    scales = lax.fori_loop(0, devices, encode_step, jnp.zeros((devices, SUB, LANES), jnp.float32), unroll=2)
    greet(devices, me)
    copies = []
    for step in range(1, devices):
        peer = lax.rem(me + step, devices)
        copies.append(send_to(devices, me, step, sendb.at[peer], recvb.at[me], send_sem.at[step], recv_sem.at[step]))
        copies[-1].start()
    ones = jnp.ones((SUB, LANES), jnp.float32)
    weighted = dot(ones, hour_sums[...], 1, 1)
    for p in range(devices):
        small_out[p] = jnp.where(iota((SUB, LANES), 0) < SUB // 2, weighted, scales[p])
    for step in range(1, devices):
        peer = lax.rem(me + step, devices)
        copies.append(
            send_to(devices, me, step, small_out.at[peer], small_in.at[me], small_send.at[step], small_recv.at[step])
        )
        copies[-1].start()
    small_in[me] = small_out[me]
    recvb[me] = sendb[me]
    time_wide = halves(spread_matrix(time_ref[...], SUB, True))
    coarse_wide = halves(spread_matrix(coarse_ref[...], chunk, True))
    fine = stacked(fine_ref[...])
    square = jnp.ones((LANES, LANES), jnp.float32)
    lat_sums = dot(square, lat_ref[...], 1, 0)
    place = (iota((rows, LANES), 1) == SUB * me + iota((rows, LANES), 0) % SUB).astype(jnp.float32)
    lat_column = dot(place, lat_sums, 1, 1)
    for copy in copies:
        copy.wait()
    total = small_in[0, 0:1]
    for p in range(1, devices):
        total = total + small_in[p, 0:1]
    level = total / totals_ref[0:1, hours:hours + 1]
    hour_of = (iota((rows, LANES), 1) == iota((rows, LANES), 0) // SUB).astype(jnp.float32)
    level_column = dot(hour_of, jnp.broadcast_to(level, (LANES, LANES)), 1, 1)
    shift = lat_column * level_column
    for p in range(devices):
        work[p] = decode(recvb[p], small_in[p, SUB - 1:SUB], chunk) - shift

    def coarse_step(r, carry):
        at = pl.ds(pl.multiple_of(r * chunk, chunk), chunk)
        mixed[:, at, :] = left_wide(coarse_wide, work[:, at, :].reshape(devices * chunk, LANES)).reshape(
            devices, chunk, LANES
        )
        return carry

    lax.fori_loop(0, devices, coarse_step, 0, unroll=2)

    def fine_step(p, carry):
        lanes = pl.ds(pl.multiple_of(p * LANES, LANES), LANES)
        out_ref[:, lanes] = x_ref[:, lanes] + left_wide(time_wide, right_square(mixed[p], fine))
        return carry

    lax.fori_loop(0, devices, fine_step, 0, unroll=2)


def f32(*shape):
    return jax.ShapeDtypeStruct(shape, jnp.float32)


def vmem(count):
    return [pl.BlockSpec(memory_space=pltpu.VMEM)] * count


def smem(count):
    return [pl.BlockSpec(memory_space=pltpu.SMEM)] * count


def by_longitude(
    control,
    prior_flux,
    area_weight,
    time_factor,
    lat_factor,
    coarse_lon,
    fine_lon,
    footprint_tiles,
    footprint_hours,
    footprint_weights,
    observations,
    error_variance,
):
    devices = lax.axis_size("cells")
    hours, lat_rows, longitude = control.shape
    latitude = lat_factor.shape[0]
    rows = hours * lat_rows
    foot = footprint_tiles.shape[1]
    slots = footprint_tiles.size
    soundings = footprint_tiles.shape[0]
    cells = hours * latitude

    tiles = footprint_tiles.reshape(-1)
    hour = footprint_hours.reshape(-1)
    lat = tiles // devices
    tile = tiles % devices
    slot = jnp.arange(slots, dtype=jnp.int32)
    by_lon = (tile * cells + hour * latitude + lat) * slots + slot
    by_lat = ((lat // lat_rows) * cells + tile * rows + hour * lat_rows + lat % lat_rows) * slots + slot
    ordered = lax.sort(jnp.stack([by_lon, by_lat]), dimension=1)
    edges = jnp.arange(LANES, dtype=jnp.int32) * (cells * slots)
    starts = jnp.sum((ordered[:, None, :] < edges[None, :, None]).astype(jnp.int32), axis=2)
    room = jnp.zeros((2, 3 * LANES), jnp.int32)
    listed = jnp.concatenate([ordered, starts, room], axis=1).reshape(-1, LANES)

    x = control.reshape(rows, longitude)
    prior = prior_flux.reshape(rows, longitude)
    sems = [pltpu.SemaphoreType.DMA((devices,))] * 4
    blocks = (devices, rows, LANES)
    limits = dict(vmem_limit_bytes=MESH_BUDGET, has_side_effects=True)
    every_list = (devices,) + listed.shape
    increment, area_column, totals, gathered, lists = pl.pallas_call(
        functools.partial(forward_kernel, devices),
        out_shape=(
            f32(cells, LANES),
            f32(latitude, LANES),
            f32(SUB, LANES),
            jax.ShapeDtypeStruct((devices, slots, LANES), jnp.bfloat16),
            jax.ShapeDtypeStruct(every_list, jnp.int32),
        ),
        in_specs=vmem(8),
        out_specs=tuple(vmem(5)),
        scratch_shapes=[
            pltpu.VMEM(blocks, jnp.float32),
            pltpu.VMEM((rows, LANES), jnp.float32),
            pltpu.VMEM(blocks, jnp.int16),
            pltpu.VMEM(blocks, jnp.int16),
            pltpu.VMEM((devices, 2 * SUB, LANES), jnp.float32),
            pltpu.VMEM((devices, 2 * SUB, LANES), jnp.float32),
            pltpu.VMEM(every_list, jnp.int32),
        ] + sems + sems,
        compiler_params=pltpu.CompilerParams(collective_id=0, **limits),
    )(footprint_weights.reshape(slots, LANES), listed, x, area_weight, time_factor, lat_factor, coarse_lon, fine_lon)

    lists = lists.reshape(-1)
    partial = pl.pallas_call(
        functools.partial(share_kernel, devices, slots, foot),
        out_shape=f32(devices, SUB, soundings),
        in_specs=smem(2) + vmem(4),
        out_specs=vmem(1)[0],
        scratch_shapes=[
            pltpu.VMEM((devices * slots, LANES), jnp.float32),
            pltpu.VMEM((cells, LANES), jnp.float32),
            pltpu.VMEM((devices * slots, LANES), jnp.float32),
        ],
        compiler_params=pltpu.CompilerParams(vmem_limit_bytes=MESH_BUDGET),
    )(lists, totals[0], gathered, increment, prior, area_weight)

    small = pltpu.VMEM((devices, SUB, LANES), jnp.float32)
    every, own = pl.pallas_call(
        functools.partial(misfit_kernel, devices),
        out_shape=(f32(devices, SUB, soundings), f32(SUB, soundings)),
        in_specs=vmem(3),
        out_specs=tuple(vmem(2)),
        scratch_shapes=[small, small, pltpu.VMEM((SUB, LANES), jnp.float32)] + sems,
        compiler_params=pltpu.CompilerParams(collective_id=1, **limits),
    )(partial, observations.reshape(1, soundings), error_variance.reshape(1, soundings))

    grad = pl.pallas_call(
        functools.partial(scatter_kernel, devices, slots, foot),
        out_shape=f32(cells, LANES),
        in_specs=smem(2) + vmem(1),
        out_specs=vmem(1)[0],
        scratch_shapes=[pltpu.VMEM((devices * slots, LANES), jnp.float32)],
        compiler_params=pltpu.CompilerParams(vmem_limit_bytes=MESH_BUDGET),
    )(lists, every[:, 0].reshape(-1), gathered)

    gradient = pl.pallas_call(
        functools.partial(adjoint_kernel, devices),
        out_shape=f32(rows, longitude),
        in_specs=vmem(8),
        out_specs=vmem(1)[0],
        scratch_shapes=[
            pltpu.VMEM(blocks, jnp.float32),
            pltpu.VMEM(blocks, jnp.float32),
            pltpu.VMEM((LANES, LANES), jnp.float32),
            pltpu.VMEM(blocks, jnp.int16),
            pltpu.VMEM(blocks, jnp.int16),
            small,
            small,
        ] + sems,
        compiler_params=pltpu.CompilerParams(collective_id=2, **limits),
    )(grad, area_column, totals, x, time_factor, lat_factor, coarse_lon, fine_lon)
    return gradient.reshape(control.shape), own[0]


def fits(devices, control, coarse_lon, fine_lon, lat_factor, footprint_tiles):
    return (
        devices == coarse_lon.shape[0]
        and devices % 4 == 0
        and fine_lon.shape[0] == LANES
        and control.shape[1] == SUB
        and lat_factor.shape[0] == LANES
        and footprint_tiles.shape[0] == LANES
        and (control.shape[0] * SUB) % (16 * devices) == 0
        and control.shape[0] < LANES
        and devices * control.shape[0] * LANES * footprint_tiles.size < 2**31
        and devices < LANES
    )


def per_device(*arrays):
    devices = lax.axis_size("cells")
    control, lat_factor, coarse_lon, fine_lon, footprint_tiles = (arrays[i] for i in (0, 4, 5, 6, 7))
    if fits(devices, control, coarse_lon, fine_lon, lat_factor, footprint_tiles):
        return by_longitude(*arrays)
    return by_latitude(*arrays)


def solution(mesh):
    placed = (
        P("ens", "cells", None),
        P(None, "cells", None),
        P("cells", None),
        P(),
        P(),
        P(),
        P(),
        P("cells", None),
        P("cells", None),
        P("cells", None, None),
        P(("ens", "cells")),
        P("cells"),
    )
    return jax.shard_map(
        per_device,
        mesh=mesh,
        in_specs=placed,
        out_specs=(P("ens", "cells", None), P(("ens", "cells"))),
        check_vma=False,
    )
```

```python
import functools

import jax
import jax.numpy as jnp
from jax import lax
from jax.experimental import pallas as pl
from jax.experimental.pallas import tpu as pltpu
from jax.sharding import PartitionSpec as P

highest = lax.Precision.HIGHEST


def lon_apply(field, coarse_lon, fine_lon):
    shaped = field.reshape(field.shape[0], field.shape[1], coarse_lon.shape[0], fine_lon.shape[0])
    shaped = jnp.einsum("hapq,fq->hapf", shaped, fine_lon, precision=highest)
    shaped = jnp.einsum("hapf,cp->hacf", shaped, coarse_lon, precision=highest)
    return shaped.reshape(field.shape)


def lon_adjoint(field, coarse_lon, fine_lon):
    shaped = field.reshape(field.shape[0], field.shape[1], coarse_lon.shape[0], fine_lon.shape[0])
    shaped = jnp.einsum("hapq,qf->hapf", shaped, fine_lon, precision=highest)
    shaped = jnp.einsum("hapf,pc->hacf", shaped, coarse_lon, precision=highest)
    return shaped.reshape(field.shape)


def time_apply(field, time_factor):
    return jnp.einsum("gh,hab->gab", time_factor, field, precision=highest)


def time_adjoint(field, time_factor):
    return jnp.einsum("hg,hab->gab", time_factor, field, precision=highest)


def lat_apply(field, lat_factor):
    return jnp.einsum("ca,hab->hcb", lat_factor, field, precision=highest)


def lat_adjoint(field, lat_factor):
    return jnp.einsum("ac,hab->hcb", lat_factor, field, precision=highest)


def to_columns(field):
    return lax.all_to_all(field, "cells", split_axis=2, concat_axis=1, tiled=True)


def to_rows(field):
    return lax.all_to_all(field, "cells", split_axis=1, concat_axis=2, tiled=True)


def by_latitude(
    control,
    prior_flux,
    area_weight,
    time_factor,
    lat_factor,
    coarse_lon,
    fine_lon,
    footprint_tiles,
    footprint_hours,
    footprint_weights,
    observations,
    error_variance,
):
    devices = lax.axis_size("cells")
    hours_count = control.shape[0]
    tile_width = footprint_weights.shape[2]
    spread = lon_apply(control, coarse_lon, fine_lon)
    spread = time_apply(spread, time_factor)
    increment = to_rows(lat_apply(to_columns(spread), lat_factor))
    hourly, total_weight = lax.psum(
        (jnp.sum(increment, axis=(1, 2)), jnp.sum(area_weight)), "cells"
    )
    flux_field = prior_flux + increment - area_weight[None] * (hourly / total_weight)[:, None, None]
    flux_rows = flux_field.astype(jnp.bfloat16).reshape(-1, tile_width)
    tile_count = flux_rows.shape[0] // hours_count
    slot_total = footprint_tiles.size
    capacity = 2 * slot_total // devices
    owners = (footprint_tiles // tile_count).reshape(-1)
    row_index = (footprint_hours * tile_count + footprint_tiles % tile_count).reshape(-1)
    order = jnp.argsort(owners, stable=True)
    sorted_owners = owners[order]
    starts = jnp.searchsorted(sorted_owners, jnp.arange(devices, dtype=jnp.int32))
    ranked = jnp.arange(slot_total, dtype=jnp.int32) - starts[sorted_owners]
    target = jnp.zeros((slot_total,), jnp.int32).at[order].set(sorted_owners * capacity + ranked)
    weights_flat = footprint_weights.reshape(slot_total, tile_width)
    request_rows = (
        jnp.zeros((devices * capacity,), jnp.int32)
        .at[target]
        .set(row_index)
        .reshape(devices, capacity)
    )
    send_weights = (
        jnp.zeros((devices * capacity, tile_width), jnp.bfloat16).at[target].set(weights_flat)
    )
    got_weights, got_rows = (
        lax.all_to_all(
            send_weights.reshape(devices, capacity, tile_width),
            "cells",
            split_axis=0,
            concat_axis=0,
            tiled=True,
        ),
        lax.all_to_all(request_rows, "cells", split_axis=0, concat_axis=0, tiled=True),
    )
    got_index = got_rows.reshape(-1)
    got_flat = got_weights.reshape(-1, tile_width)
    shares = jnp.einsum(
        "sc,sc->s", flux_rows[got_index], got_flat, preferred_element_type=jnp.float32
    )
    returned = lax.all_to_all(
        shares.reshape(devices, capacity), "cells", split_axis=0, concat_axis=0, tiled=True
    )
    predicted = returned.reshape(-1)[target].reshape(footprint_tiles.shape).sum(axis=1)
    misfit = (predicted - observations) / error_variance
    slot_misfit = jnp.broadcast_to(misfit[:, None], footprint_tiles.shape).reshape(-1)
    send_misfit = jnp.zeros((devices * capacity,), jnp.float32).at[target].set(slot_misfit)
    got_misfit = lax.all_to_all(
        send_misfit.reshape(devices, capacity), "cells", split_axis=0, concat_axis=0, tiled=True
    )
    contrib = got_flat * got_misfit.reshape(-1)[:, None]
    grad_rows = jnp.zeros(flux_rows.shape, jnp.float32).at[got_index].add(contrib)
    grad_flux = grad_rows.reshape(prior_flux.shape)
    weighted = lax.psum(jnp.sum(area_weight[None] * grad_flux, axis=(1, 2)), "cells")
    projected = grad_flux - (weighted / total_weight)[:, None, None]
    back = to_rows(lat_adjoint(to_columns(projected), lat_factor))
    back = time_adjoint(back, time_factor)
    back = lon_adjoint(back, coarse_lon, fine_lon)
    return (control + back, misfit)


MESH_BUDGET = 56 * 1024 * 1024
LANES = 128
SUB = 8


def dot(left, right, left_dim, right_dim):
    return lax.dot_general(
        left,
        right,
        (((left_dim,), (right_dim,)), ((), ())),
        precision=highest,
        preferred_element_type=jnp.float32,
    )


def iota(shape, dim):
    return lax.broadcasted_iota(jnp.int32, shape, dim)


def halves(value):
    high = value.astype(jnp.bfloat16)
    return high, (value - high.astype(jnp.float32)).astype(jnp.bfloat16)


def product(left, right):
    return lax.dot_general(left, right, (((1,), (0,)), ((), ())), preferred_element_type=jnp.float32)


def stacked(value):
    high, low = halves(value)
    above = jnp.concatenate([high, low], axis=1)
    below = jnp.concatenate([high, jnp.zeros_like(high)], axis=1)
    return jnp.concatenate([above, below], axis=0)


def fold(wide):
    return wide[:, :LANES] + wide[:, LANES:]


def left_wide(factor, data):
    high, low = halves(data)
    return fold(product(factor[0], jnp.concatenate([high, low], axis=1))) + product(factor[1], high)


def left_square(factor, data):
    return fold(product(jnp.concatenate(factor, axis=1), stacked(data)))


def right_square(data, factor):
    return fold(product(jnp.concatenate(halves(data), axis=1), factor))


def spread_matrix(factor, repeat, adjoint):
    size = factor.shape[0]
    pick = (iota((size * repeat, size), 0) // repeat == iota((size * repeat, size), 1)).astype(jnp.float32)
    wide = dot(dot(pick, factor, 1, 1 if adjoint else 0), pick, 1, 1)
    whole = (size * repeat, size * repeat)
    return jnp.where(iota(whole, 0) % repeat == iota(whole, 1) % repeat, wide, 0.0)


def encode(blocks, scales, at, out_ref, column):
    largest = jnp.maximum(jnp.max(jnp.abs(blocks), axis=(1, 2), keepdims=True), 1e-33)
    out_ref[:, at, :] = jnp.round(blocks * (32767.0 / largest)).astype(jnp.int32).astype(jnp.int16)
    return jnp.where(iota(scales.shape, 2) == column, largest * (1.0 / 32767.0), scales)


def decode(coded, steps, chunk, first):
    rows = coded.shape[0]
    pick = (iota((rows, LANES), 1) == (iota((rows, LANES), 0) + first) // chunk).astype(jnp.float32)
    return coded.astype(jnp.int32).astype(jnp.float32) * dot(pick, jnp.broadcast_to(steps, (LANES, LANES)), 1, 1)


def split(value, size):
    if size & (size - 1) == 0:
        return lax.shift_right_logical(value, size.bit_length() - 1), value & (size - 1)
    return lax.div(value, size), lax.rem(value, size)


def greet(devices, me):
    barrier = pltpu.get_barrier_semaphore()
    for step in range(1, devices):
        pl.semaphore_signal(
            barrier, inc=1, device_id={"cells": lax.rem(me + step, devices)}, device_id_type=pl.DeviceIdType.MESH
        )
    pl.semaphore_wait(barrier, devices - 1)


def send_half(devices, me, half, sendb, recvb, send_sem, recv_sem):
    rows = sendb.shape[1] // 2
    part = pl.ds(half * rows, rows)
    copies = []
    for step in range(1, devices):
        peer = lax.rem(me + step, devices)
        source, target = sendb.at[peer, part], recvb.at[me, part]
        copies.append(
            send_to(devices, me, step, source, target, send_sem.at[half, step], recv_sem.at[half, step])
        )
        copies[-1].start()
    return copies


def send_to(devices, me, step, source, target, send_sem, recv_sem):
    return pltpu.make_async_remote_copy(
        src_ref=source,
        dst_ref=target,
        send_sem=send_sem,
        recv_sem=recv_sem,
        device_id={"cells": lax.rem(me + step, devices)},
        device_id_type=pl.DeviceIdType.MESH,
    )


class Travel:
    def __init__(self, devices, me, own, everyone, send_sem, recv_sem):
        self.devices, self.me, self.own, self.everyone = devices, me, own, everyone
        self.send_sem, self.recv_sem = send_sem, recv_sem
        self.steps = devices // 4
        self.z = lax.div(me, 4)
        self.across = self.across_of(me)
        self.core = me + 1 - 2 * lax.rem(me, 2)

    def across_of(self, device):
        return device + 2 - 4 * lax.rem(lax.div(device, 2), 2)

    def behind(self, device, step):
        return lax.rem(device - 4 * step + self.devices, self.devices)

    def inside(self, z):
        return (z >= 0) & (z < self.steps)

    def copy(self, at, block, peer, lane=0):
        return pltpu.make_async_remote_copy(
            src_ref=self.everyone.at[block],
            dst_ref=self.everyone.at[block],
            send_sem=self.send_sem.at[at + lane],
            recv_sem=self.recv_sem.at[at],
            device_id={"cells": peer},
            device_id_type=pl.DeviceIdType.MESH,
        )

    def onward(self, direction, hops):
        block = self.me - 4 * direction * hops
        at, lane = (hops + 1, 0) if direction > 0 else (self.steps - 1 - hops, self.devices)
        return self.copy(at, block, self.me + 4 * direction, lane), self.inside(self.z + direction)

    def start(self):
        self.everyone[self.me] = self.own[...]
        for direction in (1, -1):
            copy, there = self.onward(direction, 0)
            pl.when(there)(copy.start)
        self.copy(self.steps, self.me, self.across).start()
        self.copy(2 * self.steps, self.me, self.core).start()

    def arrive(self, hops):
        for direction in (1, -1):
            block = self.me - 4 * direction * hops
            at = hops if direction > 0 else self.steps - hops

            @pl.when(self.inside(self.z - direction * hops))
            def _():
                self.copy(at, block, self.core).wait_recv()
                if hops < self.steps - 1:
                    copy, there = self.onward(direction, hops)
                    pl.when(there)(copy.start)
                self.copy(self.steps + at, block, self.across).start()
                self.copy(2 * self.steps + at, block, self.core).start()

    def second(self):
        for step in range(self.steps):
            block = self.behind(self.across, step)
            self.copy(self.steps + step, block, self.core).wait_recv()
            self.copy(3 * self.steps + step, block, self.core).start()

    def finish(self):
        for step in range(self.steps):
            self.copy(2 * self.steps + step, self.behind(self.core, step), self.core).wait_recv()
            self.copy(3 * self.steps + step, self.behind(self.across_of(self.core), step), self.core).wait_recv()
        for step in range(self.steps):
            block = self.behind(self.me, step)
            self.copy(self.steps + step, block, self.across).wait_send()
            self.copy(2 * self.steps + step, block, self.core).wait_send()
            self.copy(3 * self.steps + step, self.behind(self.across, step), self.core).wait_send()
        for direction in (1, -1):
            for hops in range(self.steps - 1):
                copy, there = self.onward(direction, hops)
                pl.when(there & self.inside(self.z - direction * hops))(copy.wait_send)


def forward_kernel(
    devices, weights_ref, list_ref, seen_ref, variance_ref, x_ref, area_ref, time_ref, lat_ref, coarse_ref, fine_ref,
    inc_ref, area_out, totals_ref, weights_out, list_out, seen_out, variance_out,
    work, sums, sendb, recvb, small_out, small_in, list_in, send_sem, recv_sem, small_send, small_recv,
    list_send, list_recv, travel_send, travel_recv,
):
    me = lax.axis_index("cells")
    rows = x_ref.shape[0]
    hours = time_ref.shape[0]
    chunk = rows // devices
    greet(devices, me)
    travel = Travel(devices, me, weights_ref, weights_out, travel_send, travel_recv)
    travel.start()
    copies = []
    for step in range(1, devices):
        copies.append(send_to(devices, me, step, list_ref, list_in.at[me], list_send.at[step], list_recv.at[step]))
        copies[-1].start()
    time_wide = halves(spread_matrix(time_ref[...], SUB, False))
    coarse_wide = halves(spread_matrix(coarse_ref[...], chunk, False))
    fine = stacked(fine_ref[...].T)

    def fine_step(p, carry):
        part = x_ref[:, pl.ds(pl.multiple_of(p * LANES, LANES), LANES)]
        work[p] = right_square(left_wide(time_wide, part), fine)
        return carry

    lax.fori_loop(0, devices, fine_step, 0, unroll=2)
    travel.arrive(1)

    def coarse_step(r, carry):
        at = pl.ds(pl.multiple_of(r * chunk, chunk), chunk)
        mixed = left_wide(coarse_wide, work[:, at, :].reshape(devices * chunk, LANES)).reshape(devices, chunk, LANES)
        sums[at, :] = jnp.sum(mixed, axis=0)
        return encode(mixed, carry, at, sendb, r)

    scales = jnp.zeros((devices, SUB, LANES), jnp.float32)
    sent = []
    for half in range(2):
        middle = devices // 2
        scales = lax.fori_loop(half * middle, (half + 1) * middle, coarse_step, scales, unroll=2)
        sent.append(send_half(devices, me, half, sendb, recvb, send_sem, recv_sem))
    ones = jnp.ones((SUB, LANES), jnp.float32)
    lat_sums = dot(ones, lat_ref[...], 1, 0)
    place = (iota((LANES, rows), 0) == SUB * me + iota((LANES, rows), 1) % SUB).astype(jnp.float32)
    lat_row = dot(lat_sums, place, 1, 0)[0:1]
    hour_weights = jnp.where(iota((LANES, rows), 0) == iota((LANES, rows), 1) // SUB, lat_row, 0.0)
    mine = dot(ones, dot(hour_weights, sums[...], 1, 0), 1, 1)
    area_total = jnp.sum(jnp.sum(area_ref[...], axis=1, keepdims=True), axis=0, keepdims=True)
    mine = jnp.where(iota((SUB, LANES), 1) == hours, area_total, mine)
    for p in range(devices):
        small_out[p, 0:SUB] = area_ref[:, p * LANES:(p + 1) * LANES]
        small_out[p, SUB:2 * SUB] = jnp.where(iota((SUB, LANES), 0) < SUB // 2, mine, scales[p])
        small_out[p, SUB + 1:SUB + 2] = seen_ref[...]
        small_out[p, SUB + 2:SUB + 3] = variance_ref[...]
    for step in range(1, devices):
        peer = lax.rem(me + step, devices)
        copies.append(
            send_to(devices, me, step, small_out.at[peer], small_in.at[me], small_send.at[step], small_recv.at[step])
        )
        copies[-1].start()
    recvb[me] = sendb[me]
    small_in[me] = small_out[me]
    list_in[me] = list_ref[...]
    for hops in range(2, travel.steps):
        travel.arrive(hops)
    travel.second()
    for copy in copies:
        copy.wait()
    list_out[...] = list_in[...]
    total = small_in[0, SUB:SUB + 1]
    for p in range(1, devices):
        total = total + small_in[p, SUB:SUB + 1]
    total = jnp.broadcast_to(total, (SUB, LANES))
    weight = total[:, hours:hours + 1]
    totals_ref[...] = jnp.where(iota((SUB, LANES), 1) == hours, total, total / weight)
    for p in range(devices):
        area_out[SUB * p:SUB * (p + 1), :] = small_in[p, 0:SUB]
        seen_out[p:p + 1, :] = small_in[p, SUB + 1:SUB + 2]
        variance_out[p:p + 1, :] = small_in[p, SUB + 2:SUB + 3]
    lat = halves(lat_ref[...])

    def lat_step(h, carry):
        at = pl.ds(pl.multiple_of(h * SUB, SUB), SUB)
        column = work[:, at, :].reshape(devices * SUB, LANES)
        inc_ref[pl.ds(pl.multiple_of(h * LANES, LANES), LANES), :] = left_square(lat, column)
        return carry

    for half in range(2):
        for copy in sent[half]:
            copy.wait()
        first = half * (rows // 2)
        part = slice(first, first + rows // 2)
        for p in range(devices):
            work[p, part] = decode(recvb[p, part], small_in[p, 2 * SUB - 1:2 * SUB], chunk, first)
        lax.fori_loop(half * (hours // 2), (half + 1) * (hours // 2), lat_step, 0, unroll=4)
    travel.finish()


def share_kernel(
    devices, slots, foot, lists, mean, weights_ref, inc_ref, prior_ref, area_ref, out_ref, wide, prior_rows, shares
):
    me = lax.axis_index("cells")
    rows = prior_ref.shape[0]
    soundings = slots // foot
    stride = lists.shape[0] // (2 * devices)

    def widen(s, carry):
        at = pl.ds(pl.multiple_of(s * slots, slots), slots)
        wide[at, :] = weights_ref[s].astype(jnp.float32)
        shares[at, :] = jnp.zeros((slots, LANES), jnp.float32)
        return carry

    lax.fori_loop(0, devices, widen, 0)

    def prior_step(h, carry):
        level = mean[h]
        for p in range(devices):
            lanes = slice(p * LANES, (p + 1) * LANES)
            prior_rows[pl.ds(pl.multiple_of(p * rows + h * SUB, SUB), SUB), :] = (
                prior_ref[pl.ds(pl.multiple_of(h * SUB, SUB), SUB), lanes] - area_ref[:, lanes] * level
            )
        return carry

    lax.fori_loop(0, rows // SUB, prior_step, 0)

    def each_source(which, table, add):
        def source(s, carry):
            base = (2 * s + which) * stride
            low = lists[base + slots + me]
            high = lists[base + slots + me + 1]

            def group(first, count):
                products, places = [], []
                for j in range(count):
                    value = lists[base + first + j]
                    row, slot = split(value, slots)
                    row = split(row, table.shape[0])[1]
                    sounding, k = split(slot, foot)
                    place = k * (devices * soundings) + s * soundings + sounding
                    product = table[pl.ds(row, 1), :] * wide[pl.ds(s * slots + slot, 1), :]
                    if add:
                        product = product + shares[pl.ds(place, 1), :]
                    products.append(product)
                    places.append(place)
                for place, product in zip(places, products):
                    shares[pl.ds(place, 1), :] = product

            groups = (high - low) // 8

            def full(i, inner):
                group(low + i * 8, 8)
                return inner

            def rest(i, inner):
                group(i, 1)
                return inner

            lax.fori_loop(0, groups, full, 0)
            lax.fori_loop(low + groups * 8, high, rest, 0)
            return carry

        lax.fori_loop(0, devices, source, 0)

    each_source(0, inc_ref, False)
    each_source(1, prior_rows, True)
    ones = jnp.ones((SUB, LANES), jnp.float32)

    def collect(s, carry):
        summed = shares[pl.ds(pl.multiple_of(s * soundings, soundings), soundings), :]
        for k in range(1, foot):
            at = pl.multiple_of(k * devices * soundings + s * soundings, soundings)
            summed = summed + shares[pl.ds(at, soundings), :]
        out_ref[pl.ds(s, 1), :] = dot(ones, summed, 1, 1)[0:1]
        return carry

    lax.fori_loop(0, devices, collect, 0)


def misfit_kernel(devices, part_ref, seen_ref, variance_ref, all_ref, got, send_sem, recv_sem):
    me = lax.axis_index("cells")
    greet(devices, me)
    copies = []
    for step in range(1, devices):
        copies.append(send_to(devices, me, step, part_ref, got.at[me], send_sem.at[step], recv_sem.at[step]))
        copies[-1].start()
    got[me] = part_ref[...]
    for copy in copies:
        copy.wait()
    predicted = got[0]
    for p in range(1, devices):
        predicted = predicted + got[p]
    all_ref[...] = (predicted - seen_ref[...]) / variance_ref[...]


def scatter_kernel(devices, slots, foot, lists, misfit, weights_ref, grad_ref, wide):
    me = lax.axis_index("cells")
    soundings = slots // foot
    stride = lists.shape[0] // (2 * devices)
    cells = grad_ref.shape[0]

    def widen(s, carry):
        at = pl.ds(pl.multiple_of(s * slots, slots), slots)
        wide[at, :] = weights_ref[s].astype(jnp.float32)
        part = cells // devices
        grad_ref[pl.ds(pl.multiple_of(s * part, part), part), :] = jnp.zeros((part, LANES), jnp.float32)
        return carry

    lax.fori_loop(0, devices, widen, 0)

    def source(s, carry):
        base = 2 * s * stride
        low = lists[base + slots + me]
        high = lists[base + slots + me + 1]

        def group(first, count):
            products, places = [], []
            for j in range(count):
                value = lists[base + first + j]
                row, slot = split(value, slots)
                places.append(split(row, cells)[1])
                products.append(wide[pl.ds(s * slots + slot, 1), :] * misfit[s * soundings + split(slot, foot)[0]])
            for place, product in zip(places, products):
                grad_ref[pl.ds(place, 1), :] += product

        groups = (high - low) // 8

        def full(i, inner):
            group(low + i * 8, 8)
            return inner

        def rest(i, inner):
            group(i, 1)
            return inner

        lax.fori_loop(0, groups, full, 0)
        lax.fori_loop(low + groups * 8, high, rest, 0)
        return carry

    lax.fori_loop(0, devices, source, 0)


def adjoint_kernel(
    devices, grad_ref, area_ref, totals_ref, time_ref, lat_ref, coarse_ref, fine_ref, out_ref,
    work, mixed, hour_sums, sendb, recvb, small_out, small_in, send_sem, recv_sem, small_send, small_recv,
):
    me = lax.axis_index("cells")
    rows = out_ref.shape[0]
    hours = time_ref.shape[0]
    chunk = rows // devices
    lat = halves(lat_ref[...].T)
    hour_sums[...] = jnp.zeros(hour_sums.shape, jnp.float32)

    def lat_step(h, carry):
        field = grad_ref[pl.ds(pl.multiple_of(h * LANES, LANES), LANES), :]
        at = pl.ds(pl.multiple_of(h * SUB, SUB), SUB)
        work[:, at, :] = left_square(lat, field).reshape(devices, SUB, LANES)
        hour_sums[pl.ds(h, 1), :] = jnp.sum(field * area_ref[...], axis=0, keepdims=True)
        return carry

    def encode_step(r, carry):
        at = pl.ds(pl.multiple_of(r * chunk, chunk), chunk)
        return encode(work[:, at, :], carry, at, sendb, r)

    greet(devices, me)
    scales = jnp.zeros((devices, SUB, LANES), jnp.float32)
    sent = []
    for half in range(2):
        middle = devices // 2
        lax.fori_loop(half * (hours // 2), (half + 1) * (hours // 2), lat_step, 0, unroll=4)
        scales = lax.fori_loop(half * middle, (half + 1) * middle, encode_step, scales, unroll=2)
        sent.append(send_half(devices, me, half, sendb, recvb, send_sem, recv_sem))
    copies = []
    ones = jnp.ones((SUB, LANES), jnp.float32)
    weighted = dot(ones, hour_sums[...], 1, 1)
    for p in range(devices):
        small_out[p] = jnp.where(iota((SUB, LANES), 0) < SUB // 2, weighted, scales[p])
    for step in range(1, devices):
        peer = lax.rem(me + step, devices)
        copies.append(
            send_to(devices, me, step, small_out.at[peer], small_in.at[me], small_send.at[step], small_recv.at[step])
        )
        copies[-1].start()
    small_in[me] = small_out[me]
    recvb[me] = sendb[me]
    time_wide = halves(spread_matrix(time_ref[...], SUB, True))
    coarse_wide = halves(spread_matrix(coarse_ref[...], chunk, True))
    fine = stacked(fine_ref[...])
    square = jnp.ones((LANES, LANES), jnp.float32)
    lat_sums = dot(square, lat_ref[...], 1, 0)
    place = (iota((rows, LANES), 1) == SUB * me + iota((rows, LANES), 0) % SUB).astype(jnp.float32)
    lat_column = dot(place, lat_sums, 1, 1)
    for copy in copies:
        copy.wait()
    total = small_in[0, 0:1]
    for p in range(1, devices):
        total = total + small_in[p, 0:1]
    level = total / totals_ref[0:1, hours:hours + 1]
    hour_of = (iota((rows, LANES), 1) == iota((rows, LANES), 0) // SUB).astype(jnp.float32)
    level_column = dot(hour_of, jnp.broadcast_to(level, (LANES, LANES)), 1, 1)
    shift = lat_column * level_column
    def coarse_step(r, carry):
        at = pl.ds(pl.multiple_of(r * chunk, chunk), chunk)
        mixed[:, at, :] = left_wide(coarse_wide, work[:, at, :].reshape(devices * chunk, LANES)).reshape(
            devices, chunk, LANES
        )
        return carry

    for half in range(2):
        for copy in sent[half]:
            copy.wait()
        first = half * (rows // 2)
        part = slice(first, first + rows // 2)
        for p in range(devices):
            work[p, part] = decode(recvb[p, part], small_in[p, SUB - 1:SUB], chunk, first) - shift[part]
        lax.fori_loop(half * (devices // 2), (half + 1) * (devices // 2), coarse_step, 0, unroll=2)

    def fine_step(p, carry):
        lanes = pl.ds(pl.multiple_of(p * LANES, LANES), LANES)
        out_ref[:, lanes] = left_wide(time_wide, right_square(mixed[p], fine))
        return carry

    lax.fori_loop(0, devices, fine_step, 0, unroll=2)


def f32(*shape):
    return jax.ShapeDtypeStruct(shape, jnp.float32)


def vmem(count):
    return [pl.BlockSpec(memory_space=pltpu.VMEM)] * count


def smem(count):
    return [pl.BlockSpec(memory_space=pltpu.SMEM)] * count


def by_longitude(
    control,
    prior_flux,
    area_weight,
    time_factor,
    lat_factor,
    coarse_lon,
    fine_lon,
    footprint_tiles,
    footprint_hours,
    footprint_weights,
    observations,
    error_variance,
):
    devices = lax.axis_size("cells")
    hours, lat_rows, longitude = control.shape
    latitude = lat_factor.shape[0]
    rows = hours * lat_rows
    foot = footprint_tiles.shape[1]
    slots = footprint_tiles.size
    soundings = footprint_tiles.shape[0]
    cells = hours * latitude

    tiles = footprint_tiles.reshape(-1)
    hour = footprint_hours.reshape(-1)
    lat = tiles // devices
    tile = tiles % devices
    slot = jnp.arange(slots, dtype=jnp.int32)
    by_lon = (tile * cells + hour * latitude + lat) * slots + slot
    by_lat = ((lat // lat_rows) * cells + tile * rows + hour * lat_rows + lat % lat_rows) * slots + slot
    ordered = lax.sort(jnp.stack([by_lon, by_lat]), dimension=1)
    edges = jnp.arange(LANES, dtype=jnp.int32) * (cells * slots)
    starts = jnp.sum((ordered[:, None, :] < edges[None, :, None]).astype(jnp.int32), axis=2)
    room = jnp.zeros((2, 3 * LANES), jnp.int32)
    listed = jnp.concatenate([ordered, starts, room], axis=1).reshape(-1, LANES)

    x = control.reshape(rows, longitude)
    prior = prior_flux.reshape(rows, longitude)
    pair = [pltpu.SemaphoreType.DMA((devices,))] * 2
    sems = [pltpu.SemaphoreType.DMA((2, devices))] * 2 + pair
    seen = observations.reshape(1, soundings)
    variance = error_variance.reshape(1, soundings)
    blocks = (devices, rows, LANES)
    limits = dict(vmem_limit_bytes=MESH_BUDGET, has_side_effects=True)
    every_list = (devices,) + listed.shape
    increment, area_column, totals, gathered, lists, every_seen, every_variance = pl.pallas_call(
        functools.partial(forward_kernel, devices),
        out_shape=(
            f32(cells, LANES),
            f32(latitude, LANES),
            f32(SUB, LANES),
            jax.ShapeDtypeStruct((devices, slots, LANES), jnp.bfloat16),
            jax.ShapeDtypeStruct(every_list, jnp.int32),
            f32(devices, soundings),
            f32(devices, soundings),
        ),
        in_specs=vmem(10),
        out_specs=tuple(vmem(7)),
        scratch_shapes=[
            pltpu.VMEM(blocks, jnp.float32),
            pltpu.VMEM((rows, LANES), jnp.float32),
            pltpu.VMEM(blocks, jnp.int16),
            pltpu.VMEM(blocks, jnp.int16),
            pltpu.VMEM((devices, 2 * SUB, LANES), jnp.float32),
            pltpu.VMEM((devices, 2 * SUB, LANES), jnp.float32),
            pltpu.VMEM(every_list, jnp.int32),
        ] + sems + pair + [pltpu.SemaphoreType.DMA((2 * devices,))] * 2,
        compiler_params=pltpu.CompilerParams(collective_id=0, **limits),
    )(footprint_weights.reshape(slots, LANES), listed, seen, variance, x, area_weight, time_factor, lat_factor, coarse_lon, fine_lon)

    lists = lists.reshape(-1)
    partial = pl.pallas_call(
        functools.partial(share_kernel, devices, slots, foot),
        out_shape=f32(devices, soundings),
        in_specs=smem(2) + vmem(4),
        out_specs=vmem(1)[0],
        scratch_shapes=[
            pltpu.VMEM((devices * slots, LANES), jnp.float32),
            pltpu.VMEM((cells, LANES), jnp.float32),
            pltpu.VMEM((devices * slots, LANES), jnp.float32),
        ],
        compiler_params=pltpu.CompilerParams(vmem_limit_bytes=MESH_BUDGET),
    )(lists, totals[0], gathered, increment, prior, area_weight)

    small = pltpu.VMEM((devices, SUB, LANES), jnp.float32)
    every = pl.pallas_call(
        functools.partial(misfit_kernel, devices),
        out_shape=f32(devices, soundings),
        in_specs=vmem(3),
        out_specs=vmem(1)[0],
        scratch_shapes=[pltpu.VMEM((devices, devices, soundings), jnp.float32)] + pair,
        compiler_params=pltpu.CompilerParams(collective_id=1, **limits),
    )(partial, every_seen, every_variance)

    grad = pl.pallas_call(
        functools.partial(scatter_kernel, devices, slots, foot),
        out_shape=f32(cells, LANES),
        in_specs=smem(2) + vmem(1),
        out_specs=vmem(1)[0],
        scratch_shapes=[pltpu.VMEM((devices * slots, LANES), jnp.float32)],
        compiler_params=pltpu.CompilerParams(vmem_limit_bytes=MESH_BUDGET),
    )(lists, every.reshape(-1), gathered)

    back = pl.pallas_call(
        functools.partial(adjoint_kernel, devices),
        out_shape=f32(rows, longitude),
        in_specs=vmem(7),
        out_specs=vmem(1)[0],
        scratch_shapes=[
            pltpu.VMEM(blocks, jnp.float32),
            pltpu.VMEM(blocks, jnp.float32),
            pltpu.VMEM((LANES, LANES), jnp.float32),
            pltpu.VMEM(blocks, jnp.int16),
            pltpu.VMEM(blocks, jnp.int16),
            small,
            small,
        ] + sems,
        compiler_params=pltpu.CompilerParams(collective_id=2, **limits),
    )(grad, area_column, totals, time_factor, lat_factor, coarse_lon, fine_lon)
    own = lax.dynamic_index_in_dim(every, lax.axis_index("cells"), keepdims=False)
    return control + back.reshape(control.shape), own


def fits(devices, control, coarse_lon, fine_lon, lat_factor, footprint_tiles):
    return (
        devices == coarse_lon.shape[0]
        and devices % 4 == 0
        and fine_lon.shape[0] == LANES
        and control.shape[1] == SUB
        and lat_factor.shape[0] == LANES
        and footprint_tiles.shape[0] == LANES
        and (control.shape[0] * SUB) % (16 * devices) == 0
        and control.shape[0] < LANES
        and devices * control.shape[0] * LANES * footprint_tiles.size < 2**31
        and devices < LANES
    )


def per_device(*arrays):
    devices = lax.axis_size("cells")
    control, lat_factor, coarse_lon, fine_lon, footprint_tiles = (arrays[i] for i in (0, 4, 5, 6, 7))
    if fits(devices, control, coarse_lon, fine_lon, lat_factor, footprint_tiles):
        return by_longitude(*arrays)
    return by_latitude(*arrays)


def solution(mesh):
    placed = (
        P("ens", "cells", None),
        P(None, "cells", None),
        P("cells", None),
        P(),
        P(),
        P(),
        P(),
        P("cells", None),
        P("cells", None),
        P("cells", None, None),
        P(("ens", "cells")),
        P("cells"),
    )
    return jax.shard_map(
        per_device,
        mesh=mesh,
        in_specs=placed,
        out_specs=(P("ens", "cells", None), P(("ens", "cells"))),
        check_vma=False,
    )
```

```python
import functools

import jax
import jax.numpy as jnp
from jax import lax
from jax.experimental import pallas as pl
from jax.experimental.pallas import tpu as pltpu
from jax.sharding import PartitionSpec as P

highest = lax.Precision.HIGHEST


def lon_apply(field, coarse_lon, fine_lon):
    shaped = field.reshape(field.shape[0], field.shape[1], coarse_lon.shape[0], fine_lon.shape[0])
    shaped = jnp.einsum("hapq,fq->hapf", shaped, fine_lon, precision=highest)
    shaped = jnp.einsum("hapf,cp->hacf", shaped, coarse_lon, precision=highest)
    return shaped.reshape(field.shape)


def lon_adjoint(field, coarse_lon, fine_lon):
    shaped = field.reshape(field.shape[0], field.shape[1], coarse_lon.shape[0], fine_lon.shape[0])
    shaped = jnp.einsum("hapq,qf->hapf", shaped, fine_lon, precision=highest)
    shaped = jnp.einsum("hapf,pc->hacf", shaped, coarse_lon, precision=highest)
    return shaped.reshape(field.shape)


def time_apply(field, time_factor):
    return jnp.einsum("gh,hab->gab", time_factor, field, precision=highest)


def time_adjoint(field, time_factor):
    return jnp.einsum("hg,hab->gab", time_factor, field, precision=highest)


def lat_apply(field, lat_factor):
    return jnp.einsum("ca,hab->hcb", lat_factor, field, precision=highest)


def lat_adjoint(field, lat_factor):
    return jnp.einsum("ac,hab->hcb", lat_factor, field, precision=highest)


def to_columns(field):
    return lax.all_to_all(field, "cells", split_axis=2, concat_axis=1, tiled=True)


def to_rows(field):
    return lax.all_to_all(field, "cells", split_axis=1, concat_axis=2, tiled=True)


def by_latitude(
    control,
    prior_flux,
    area_weight,
    time_factor,
    lat_factor,
    coarse_lon,
    fine_lon,
    footprint_tiles,
    footprint_hours,
    footprint_weights,
    observations,
    error_variance,
):
    devices = lax.axis_size("cells")
    hours_count = control.shape[0]
    tile_width = footprint_weights.shape[2]
    spread = lon_apply(control, coarse_lon, fine_lon)
    spread = time_apply(spread, time_factor)
    increment = to_rows(lat_apply(to_columns(spread), lat_factor))
    hourly, total_weight = lax.psum(
        (jnp.sum(increment, axis=(1, 2)), jnp.sum(area_weight)), "cells"
    )
    flux_field = prior_flux + increment - area_weight[None] * (hourly / total_weight)[:, None, None]
    flux_rows = flux_field.astype(jnp.bfloat16).reshape(-1, tile_width)
    tile_count = flux_rows.shape[0] // hours_count
    slot_total = footprint_tiles.size
    capacity = 2 * slot_total // devices
    owners = (footprint_tiles // tile_count).reshape(-1)
    row_index = (footprint_hours * tile_count + footprint_tiles % tile_count).reshape(-1)
    order = jnp.argsort(owners, stable=True)
    sorted_owners = owners[order]
    starts = jnp.searchsorted(sorted_owners, jnp.arange(devices, dtype=jnp.int32))
    ranked = jnp.arange(slot_total, dtype=jnp.int32) - starts[sorted_owners]
    target = jnp.zeros((slot_total,), jnp.int32).at[order].set(sorted_owners * capacity + ranked)
    weights_flat = footprint_weights.reshape(slot_total, tile_width)
    request_rows = (
        jnp.zeros((devices * capacity,), jnp.int32)
        .at[target]
        .set(row_index)
        .reshape(devices, capacity)
    )
    send_weights = (
        jnp.zeros((devices * capacity, tile_width), jnp.bfloat16).at[target].set(weights_flat)
    )
    got_weights, got_rows = (
        lax.all_to_all(
            send_weights.reshape(devices, capacity, tile_width),
            "cells",
            split_axis=0,
            concat_axis=0,
            tiled=True,
        ),
        lax.all_to_all(request_rows, "cells", split_axis=0, concat_axis=0, tiled=True),
    )
    got_index = got_rows.reshape(-1)
    got_flat = got_weights.reshape(-1, tile_width)
    shares = jnp.einsum(
        "sc,sc->s", flux_rows[got_index], got_flat, preferred_element_type=jnp.float32
    )
    returned = lax.all_to_all(
        shares.reshape(devices, capacity), "cells", split_axis=0, concat_axis=0, tiled=True
    )
    predicted = returned.reshape(-1)[target].reshape(footprint_tiles.shape).sum(axis=1)
    misfit = (predicted - observations) / error_variance
    slot_misfit = jnp.broadcast_to(misfit[:, None], footprint_tiles.shape).reshape(-1)
    send_misfit = jnp.zeros((devices * capacity,), jnp.float32).at[target].set(slot_misfit)
    got_misfit = lax.all_to_all(
        send_misfit.reshape(devices, capacity), "cells", split_axis=0, concat_axis=0, tiled=True
    )
    contrib = got_flat * got_misfit.reshape(-1)[:, None]
    grad_rows = jnp.zeros(flux_rows.shape, jnp.float32).at[got_index].add(contrib)
    grad_flux = grad_rows.reshape(prior_flux.shape)
    weighted = lax.psum(jnp.sum(area_weight[None] * grad_flux, axis=(1, 2)), "cells")
    projected = grad_flux - (weighted / total_weight)[:, None, None]
    back = to_rows(lat_adjoint(to_columns(projected), lat_factor))
    back = time_adjoint(back, time_factor)
    back = lon_adjoint(back, coarse_lon, fine_lon)
    return (control + back, misfit)


MESH_BUDGET = 56 * 1024 * 1024
LANES = 128
SUB = 8


def dot(left, right, left_dim, right_dim):
    return lax.dot_general(
        left,
        right,
        (((left_dim,), (right_dim,)), ((), ())),
        precision=highest,
        preferred_element_type=jnp.float32,
    )


def iota(shape, dim):
    return lax.broadcasted_iota(jnp.int32, shape, dim)


def halves(value):
    high = value.astype(jnp.bfloat16)
    return high, (value - high.astype(jnp.float32)).astype(jnp.bfloat16)


def product(left, right):
    return lax.dot_general(left, right, (((1,), (0,)), ((), ())), preferred_element_type=jnp.float32)


def stacked(value):
    high, low = halves(value)
    above = jnp.concatenate([high, low], axis=1)
    below = jnp.concatenate([high, jnp.zeros_like(high)], axis=1)
    return jnp.concatenate([above, below], axis=0)


def fold(wide):
    return wide[:, :LANES] + wide[:, LANES:]


def left_wide(factor, data):
    high, low = halves(data)
    return fold(product(factor[0], jnp.concatenate([high, low], axis=1))) + product(factor[1], high)


def left_square(factor, data):
    return fold(product(jnp.concatenate(factor, axis=1), stacked(data)))


def right_square(data, factor):
    return fold(product(jnp.concatenate(halves(data), axis=1), factor))


def spread_matrix(factor, repeat, adjoint):
    size = factor.shape[0]
    pick = (iota((size * repeat, size), 0) // repeat == iota((size * repeat, size), 1)).astype(jnp.float32)
    wide = dot(dot(pick, factor, 1, 1 if adjoint else 0), pick, 1, 1)
    whole = (size * repeat, size * repeat)
    return jnp.where(iota(whole, 0) % repeat == iota(whole, 1) % repeat, wide, 0.0)


def encode(blocks, scales, at, out_ref, column):
    largest = jnp.maximum(jnp.max(jnp.abs(blocks), axis=(1, 2), keepdims=True), 1e-33)
    out_ref[:, at, :] = jnp.round(blocks * (32767.0 / largest)).astype(jnp.int32).astype(jnp.int16)
    return jnp.where(iota(scales.shape, 2) == column, largest * (1.0 / 32767.0), scales)


def decode(coded, steps, chunk, first):
    values = coded.astype(jnp.int32).astype(jnp.float32)
    parts = []
    for at in range(0, coded.shape[0], chunk):
        column = (first + at) // chunk
        parts.append(values[at:at + chunk] * steps[:, column:column + 1])
    return jnp.concatenate(parts, axis=0)


def split(value, size):
    if size & (size - 1) == 0:
        return lax.shift_right_logical(value, size.bit_length() - 1), value & (size - 1)
    return lax.div(value, size), lax.rem(value, size)


def greet(devices, me):
    barrier = pltpu.get_barrier_semaphore()
    for step in range(1, devices):
        pl.semaphore_signal(
            barrier, inc=1, device_id={"cells": lax.rem(me + step, devices)}, device_id_type=pl.DeviceIdType.MESH
        )
    pl.semaphore_wait(barrier, devices - 1)


def send_half(devices, me, half, sendb, recvb, send_sem, recv_sem):
    rows = sendb.shape[1] // 2
    part = pl.ds(half * rows, rows)
    copies = []
    for step in range(1, devices):
        peer = lax.rem(me + step, devices)
        source, target = sendb.at[peer, part], recvb.at[me, part]
        copies.append(
            send_to(devices, me, step, source, target, send_sem.at[half, step], recv_sem.at[half, step])
        )
        copies[-1].start()
    return copies


def send_to(devices, me, step, source, target, send_sem, recv_sem):
    return pltpu.make_async_remote_copy(
        src_ref=source,
        dst_ref=target,
        send_sem=send_sem,
        recv_sem=recv_sem,
        device_id={"cells": lax.rem(me + step, devices)},
        device_id_type=pl.DeviceIdType.MESH,
    )


class Travel:
    def __init__(self, devices, me, own, everyone, send_sem, recv_sem):
        self.devices, self.me, self.own, self.everyone = devices, me, own, everyone
        self.send_sem, self.recv_sem = send_sem, recv_sem
        self.steps = devices // 4
        self.z = lax.div(me, 4)
        self.across = self.across_of(me)
        self.core = me + 1 - 2 * lax.rem(me, 2)

    def across_of(self, device):
        return device + 2 - 4 * lax.rem(lax.div(device, 2), 2)

    def behind(self, device, step):
        return lax.rem(device - 4 * step + self.devices, self.devices)

    def inside(self, z):
        return (z >= 0) & (z < self.steps)

    def copy(self, at, block, peer, lane=0):
        return pltpu.make_async_remote_copy(
            src_ref=self.everyone.at[block],
            dst_ref=self.everyone.at[block],
            send_sem=self.send_sem.at[at + lane],
            recv_sem=self.recv_sem.at[at],
            device_id={"cells": peer},
            device_id_type=pl.DeviceIdType.MESH,
        )

    def onward(self, direction, hops):
        block = self.me - 4 * direction * hops
        at, lane = (hops + 1, 0) if direction > 0 else (self.steps - 1 - hops, self.devices)
        return self.copy(at, block, self.me + 4 * direction, lane), self.inside(self.z + direction)

    def start(self):
        self.everyone[self.me] = self.own[...]
        for direction in (1, -1):
            copy, there = self.onward(direction, 0)
            pl.when(there)(copy.start)
        self.copy(self.steps, self.me, self.across).start()
        self.copy(2 * self.steps, self.me, self.core).start()

    def arrive(self, hops):
        for direction in (1, -1):
            block = self.me - 4 * direction * hops
            at = hops if direction > 0 else self.steps - hops

            @pl.when(self.inside(self.z - direction * hops))
            def _():
                self.copy(at, block, self.core).wait_recv()
                if hops < self.steps - 1:
                    copy, there = self.onward(direction, hops)
                    pl.when(there)(copy.start)
                self.copy(self.steps + at, block, self.across).start()
                self.copy(2 * self.steps + at, block, self.core).start()

    def second(self):
        for step in range(self.steps):
            block = self.behind(self.across, step)
            self.copy(self.steps + step, block, self.core).wait_recv()
            self.copy(3 * self.steps + step, block, self.core).start()

    def finish(self):
        for step in range(self.steps):
            self.copy(2 * self.steps + step, self.behind(self.core, step), self.core).wait_recv()
            self.copy(3 * self.steps + step, self.behind(self.across_of(self.core), step), self.core).wait_recv()
        for step in range(self.steps):
            block = self.behind(self.me, step)
            self.copy(self.steps + step, block, self.across).wait_send()
            self.copy(2 * self.steps + step, block, self.core).wait_send()
            self.copy(3 * self.steps + step, self.behind(self.across, step), self.core).wait_send()
        for direction in (1, -1):
            for hops in range(self.steps - 1):
                copy, there = self.onward(direction, hops)
                pl.when(there & self.inside(self.z - direction * hops))(copy.wait_send)


def forward_kernel(
    devices, weights_ref, list_ref, seen_ref, variance_ref, x_ref, area_ref, time_ref, lat_ref, coarse_ref, fine_ref,
    inc_ref, area_out, totals_ref, weights_out, list_out, seen_out, variance_out,
    work, sums, sendb, recvb, small_out, small_in, list_in, send_sem, recv_sem, small_send, small_recv,
    list_send, list_recv, travel_send, travel_recv,
):
    me = lax.axis_index("cells")
    rows = x_ref.shape[0]
    hours = time_ref.shape[0]
    chunk = rows // devices
    greet(devices, me)
    travel = Travel(devices, me, weights_ref, weights_out, travel_send, travel_recv)
    travel.start()
    copies = []
    for step in range(1, devices):
        copies.append(send_to(devices, me, step, list_ref, list_in.at[me], list_send.at[step], list_recv.at[step]))
        copies[-1].start()
    time_wide = halves(spread_matrix(time_ref[...], SUB, False))
    coarse_wide = halves(spread_matrix(coarse_ref[...], chunk, False))
    fine = stacked(fine_ref[...].T)

    def fine_step(p, carry):
        part = x_ref[:, pl.ds(pl.multiple_of(p * LANES, LANES), LANES)]
        work[p] = right_square(left_wide(time_wide, part), fine)
        return carry

    lax.fori_loop(0, devices, fine_step, 0, unroll=2)
    travel.arrive(1)

    def coarse_step(r, carry):
        at = pl.ds(pl.multiple_of(r * chunk, chunk), chunk)
        mixed = left_wide(coarse_wide, work[:, at, :].reshape(devices * chunk, LANES)).reshape(devices, chunk, LANES)
        sums[at, :] = jnp.sum(mixed, axis=0)
        return encode(mixed, carry, at, sendb, r)

    scales = jnp.zeros((devices, SUB, LANES), jnp.float32)
    sent = []
    for half in range(2):
        middle = devices // 2
        scales = lax.fori_loop(half * middle, (half + 1) * middle, coarse_step, scales, unroll=2)
        sent.append(send_half(devices, me, half, sendb, recvb, send_sem, recv_sem))
    ones = jnp.ones((SUB, LANES), jnp.float32)
    lat_sums = dot(ones, lat_ref[...], 1, 0)
    place = (iota((LANES, rows), 0) == SUB * me + iota((LANES, rows), 1) % SUB).astype(jnp.float32)
    lat_row = dot(lat_sums, place, 1, 0)[0:1]
    hour_weights = jnp.where(iota((LANES, rows), 0) == iota((LANES, rows), 1) // SUB, lat_row, 0.0)
    mine = dot(ones, dot(hour_weights, sums[...], 1, 0), 1, 1)
    area_total = jnp.sum(jnp.sum(area_ref[...], axis=1, keepdims=True), axis=0, keepdims=True)
    mine = jnp.where(iota((SUB, LANES), 1) == hours, area_total, mine)
    for p in range(devices):
        small_out[p, 0:SUB] = area_ref[:, p * LANES:(p + 1) * LANES]
        small_out[p, SUB:2 * SUB] = jnp.where(iota((SUB, LANES), 0) < SUB // 2, mine, scales[p])
        small_out[p, SUB + 1:SUB + 2] = seen_ref[...]
        small_out[p, SUB + 2:SUB + 3] = variance_ref[...]
    for step in range(1, devices):
        peer = lax.rem(me + step, devices)
        copies.append(
            send_to(devices, me, step, small_out.at[peer], small_in.at[me], small_send.at[step], small_recv.at[step])
        )
        copies[-1].start()
    recvb[me] = sendb[me]
    small_in[me] = small_out[me]
    list_in[me] = list_ref[...]
    for hops in range(2, travel.steps):
        travel.arrive(hops)
    for copy in copies:
        copy.wait()
    list_out[...] = list_in[...]
    total = small_in[0, SUB:SUB + 1]
    for p in range(1, devices):
        total = total + small_in[p, SUB:SUB + 1]
    total = jnp.broadcast_to(total, (SUB, LANES))
    weight = total[:, hours:hours + 1]
    totals_ref[...] = jnp.where(iota((SUB, LANES), 1) == hours, total, total / weight)
    for p in range(devices):
        area_out[SUB * p:SUB * (p + 1), :] = small_in[p, 0:SUB]
        seen_out[p:p + 1, :] = small_in[p, SUB + 1:SUB + 2]
        variance_out[p:p + 1, :] = small_in[p, SUB + 2:SUB + 3]
    lat = halves(lat_ref[...])

    def lat_step(h, carry):
        at = pl.ds(pl.multiple_of(h * SUB, SUB), SUB)
        column = work[:, at, :].reshape(devices * SUB, LANES)
        inc_ref[pl.ds(pl.multiple_of(h * LANES, LANES), LANES), :] = left_square(lat, column)
        return carry

    for half in range(2):
        for copy in sent[half]:
            copy.wait()
        first = half * (rows // 2)
        part = slice(first, first + rows // 2)
        for p in range(devices):
            work[p, part] = decode(recvb[p, part], small_in[p, 2 * SUB - 1:2 * SUB], chunk, first)
        lax.fori_loop(half * (hours // 2), (half + 1) * (hours // 2), lat_step, 0, unroll=4)
        if half == 0:
            travel.second()
    travel.finish()


def share_kernel(
    devices, slots, foot, lists, mean, weights_ref, inc_ref, prior_ref, area_ref, out_ref, wide, prior_rows, shares
):
    me = lax.axis_index("cells")
    rows = prior_ref.shape[0]
    soundings = slots // foot
    stride = lists.shape[0] // (2 * devices)

    def widen(s, carry):
        at = pl.ds(pl.multiple_of(s * slots, slots), slots)
        wide[at, :] = weights_ref[s].astype(jnp.float32)
        shares[at, :] = jnp.zeros((slots, LANES), jnp.float32)
        return carry

    lax.fori_loop(0, devices, widen, 0)

    def prior_step(h, carry):
        level = mean[h]
        for p in range(devices):
            lanes = slice(p * LANES, (p + 1) * LANES)
            prior_rows[pl.ds(pl.multiple_of(p * rows + h * SUB, SUB), SUB), :] = (
                prior_ref[pl.ds(pl.multiple_of(h * SUB, SUB), SUB), lanes] - area_ref[:, lanes] * level
            )
        return carry

    lax.fori_loop(0, rows // SUB, prior_step, 0)

    def each_source(which, table, add):
        def source(s, carry):
            base = (2 * s + which) * stride
            low = lists[base + slots + me]
            high = lists[base + slots + me + 1]

            def group(first, count):
                products, places = [], []
                for j in range(count):
                    value = lists[base + first + j]
                    row, slot = split(value, slots)
                    row = split(row, table.shape[0])[1]
                    sounding, k = split(slot, foot)
                    place = k * (devices * soundings) + s * soundings + sounding
                    product = table[pl.ds(row, 1), :] * wide[pl.ds(s * slots + slot, 1), :]
                    if add:
                        product = product + shares[pl.ds(place, 1), :]
                    products.append(product)
                    places.append(place)
                for place, product in zip(places, products):
                    shares[pl.ds(place, 1), :] = product

            groups = (high - low) // 8

            def full(i, inner):
                group(low + i * 8, 8)
                return inner

            def rest(i, inner):
                group(i, 1)
                return inner

            lax.fori_loop(0, groups, full, 0)
            lax.fori_loop(low + groups * 8, high, rest, 0)
            return carry

        lax.fori_loop(0, devices, source, 0)

    each_source(0, inc_ref, False)
    each_source(1, prior_rows, True)
    ones = jnp.ones((SUB, LANES), jnp.float32)

    def collect(s, carry):
        summed = shares[pl.ds(pl.multiple_of(s * soundings, soundings), soundings), :]
        for k in range(1, foot):
            at = pl.multiple_of(k * devices * soundings + s * soundings, soundings)
            summed = summed + shares[pl.ds(at, soundings), :]
        out_ref[pl.ds(s, 1), :] = dot(ones, summed, 1, 1)[0:1]
        return carry

    lax.fori_loop(0, devices, collect, 0)


def misfit_kernel(devices, part_ref, seen_ref, variance_ref, all_ref, got, send_sem, recv_sem):
    me = lax.axis_index("cells")
    greet(devices, me)
    copies = []
    for step in range(1, devices):
        copies.append(send_to(devices, me, step, part_ref, got.at[me], send_sem.at[step], recv_sem.at[step]))
        copies[-1].start()
    got[me] = part_ref[...]
    for copy in copies:
        copy.wait()
    predicted = got[0]
    for p in range(1, devices):
        predicted = predicted + got[p]
    all_ref[...] = (predicted - seen_ref[...]) / variance_ref[...]


def scatter_kernel(devices, slots, foot, lists, misfit, weights_ref, grad_ref, wide):
    me = lax.axis_index("cells")
    soundings = slots // foot
    stride = lists.shape[0] // (2 * devices)
    cells = grad_ref.shape[0]

    def widen(s, carry):
        at = pl.ds(pl.multiple_of(s * slots, slots), slots)
        wide[at, :] = weights_ref[s].astype(jnp.float32)
        part = cells // devices
        grad_ref[pl.ds(pl.multiple_of(s * part, part), part), :] = jnp.zeros((part, LANES), jnp.float32)
        return carry

    lax.fori_loop(0, devices, widen, 0)

    def source(s, carry):
        base = 2 * s * stride
        low = lists[base + slots + me]
        high = lists[base + slots + me + 1]

        def group(first, count):
            products, places = [], []
            for j in range(count):
                value = lists[base + first + j]
                row, slot = split(value, slots)
                places.append(split(row, cells)[1])
                products.append(wide[pl.ds(s * slots + slot, 1), :] * misfit[s * soundings + split(slot, foot)[0]])
            for place, product in zip(places, products):
                grad_ref[pl.ds(place, 1), :] += product

        groups = (high - low) // 8

        def full(i, inner):
            group(low + i * 8, 8)
            return inner

        def rest(i, inner):
            group(i, 1)
            return inner

        lax.fori_loop(0, groups, full, 0)
        lax.fori_loop(low + groups * 8, high, rest, 0)
        return carry

    lax.fori_loop(0, devices, source, 0)


def adjoint_kernel(
    devices, grad_ref, area_ref, totals_ref, time_ref, lat_ref, coarse_ref, fine_ref, out_ref,
    work, mixed, hour_sums, sendb, recvb, small_out, small_in, send_sem, recv_sem, small_send, small_recv,
):
    me = lax.axis_index("cells")
    rows = out_ref.shape[0]
    hours = time_ref.shape[0]
    chunk = rows // devices
    lat = halves(lat_ref[...].T)
    hour_sums[...] = jnp.zeros(hour_sums.shape, jnp.float32)

    def lat_step(h, carry):
        field = grad_ref[pl.ds(pl.multiple_of(h * LANES, LANES), LANES), :]
        at = pl.ds(pl.multiple_of(h * SUB, SUB), SUB)
        work[:, at, :] = left_square(lat, field).reshape(devices, SUB, LANES)
        hour_sums[pl.ds(h, 1), :] = jnp.sum(field * area_ref[...], axis=0, keepdims=True)
        return carry

    def encode_step(r, carry):
        at = pl.ds(pl.multiple_of(r * chunk, chunk), chunk)
        return encode(work[:, at, :], carry, at, sendb, r)

    greet(devices, me)
    scales = jnp.zeros((devices, SUB, LANES), jnp.float32)
    sent = []
    for half in range(2):
        middle = devices // 2
        lax.fori_loop(half * (hours // 2), (half + 1) * (hours // 2), lat_step, 0, unroll=4)
        scales = lax.fori_loop(half * middle, (half + 1) * middle, encode_step, scales, unroll=2)
        sent.append(send_half(devices, me, half, sendb, recvb, send_sem, recv_sem))
    copies = []
    ones = jnp.ones((SUB, LANES), jnp.float32)
    weighted = dot(ones, hour_sums[...], 1, 1)
    for p in range(devices):
        small_out[p] = jnp.where(iota((SUB, LANES), 0) < SUB // 2, weighted, scales[p])
    for step in range(1, devices):
        peer = lax.rem(me + step, devices)
        copies.append(
            send_to(devices, me, step, small_out.at[peer], small_in.at[me], small_send.at[step], small_recv.at[step])
        )
        copies[-1].start()
    small_in[me] = small_out[me]
    recvb[me] = sendb[me]
    time_wide = halves(spread_matrix(time_ref[...], SUB, True))
    coarse_wide = halves(spread_matrix(coarse_ref[...], chunk, True))
    fine = stacked(fine_ref[...])
    square = jnp.ones((LANES, LANES), jnp.float32)
    lat_sums = dot(square, lat_ref[...], 1, 0)
    place = (iota((rows, LANES), 1) == SUB * me + iota((rows, LANES), 0) % SUB).astype(jnp.float32)
    lat_column = dot(place, lat_sums, 1, 1)
    for copy in copies:
        copy.wait()
    total = small_in[0, 0:1]
    for p in range(1, devices):
        total = total + small_in[p, 0:1]
    level = total / totals_ref[0:1, hours:hours + 1]
    hour_of = (iota((rows, LANES), 1) == iota((rows, LANES), 0) // SUB).astype(jnp.float32)
    level_column = dot(hour_of, jnp.broadcast_to(level, (LANES, LANES)), 1, 1)
    shift = lat_column * level_column
    def coarse_step(r, carry):
        at = pl.ds(pl.multiple_of(r * chunk, chunk), chunk)
        mixed[:, at, :] = left_wide(coarse_wide, work[:, at, :].reshape(devices * chunk, LANES)).reshape(
            devices, chunk, LANES
        )
        return carry

    for half in range(2):
        for copy in sent[half]:
            copy.wait()
        first = half * (rows // 2)
        part = slice(first, first + rows // 2)
        for p in range(devices):
            work[p, part] = decode(recvb[p, part], small_in[p, SUB - 1:SUB], chunk, first) - shift[part]
        lax.fori_loop(half * (devices // 2), (half + 1) * (devices // 2), coarse_step, 0, unroll=2)

    def fine_step(p, carry):
        lanes = pl.ds(pl.multiple_of(p * LANES, LANES), LANES)
        out_ref[:, lanes] = left_wide(time_wide, right_square(mixed[p], fine))
        return carry

    lax.fori_loop(0, devices, fine_step, 0, unroll=2)


def f32(*shape):
    return jax.ShapeDtypeStruct(shape, jnp.float32)


def vmem(count):
    return [pl.BlockSpec(memory_space=pltpu.VMEM)] * count


def smem(count):
    return [pl.BlockSpec(memory_space=pltpu.SMEM)] * count


def by_longitude(
    control,
    prior_flux,
    area_weight,
    time_factor,
    lat_factor,
    coarse_lon,
    fine_lon,
    footprint_tiles,
    footprint_hours,
    footprint_weights,
    observations,
    error_variance,
):
    devices = lax.axis_size("cells")
    hours, lat_rows, longitude = control.shape
    latitude = lat_factor.shape[0]
    rows = hours * lat_rows
    foot = footprint_tiles.shape[1]
    slots = footprint_tiles.size
    soundings = footprint_tiles.shape[0]
    cells = hours * latitude

    tiles = footprint_tiles.reshape(-1)
    hour = footprint_hours.reshape(-1)
    lat = tiles // devices
    tile = tiles % devices
    slot = jnp.arange(slots, dtype=jnp.int32)
    by_lon = (tile * cells + hour * latitude + lat) * slots + slot
    by_lat = ((lat // lat_rows) * cells + tile * rows + hour * lat_rows + lat % lat_rows) * slots + slot
    ordered = lax.sort(jnp.stack([by_lon, by_lat]), dimension=1)
    edges = jnp.arange(LANES, dtype=jnp.int32) * (cells * slots)
    starts = jnp.sum((ordered[:, None, :] < edges[None, :, None]).astype(jnp.int32), axis=2)
    room = jnp.zeros((2, 3 * LANES), jnp.int32)
    listed = jnp.concatenate([ordered, starts, room], axis=1).reshape(-1, LANES)

    x = control.reshape(rows, longitude)
    prior = prior_flux.reshape(rows, longitude)
    pair = [pltpu.SemaphoreType.DMA((devices,))] * 2
    sems = [pltpu.SemaphoreType.DMA((2, devices))] * 2 + pair
    seen = observations.reshape(1, soundings)
    variance = error_variance.reshape(1, soundings)
    blocks = (devices, rows, LANES)
    limits = dict(vmem_limit_bytes=MESH_BUDGET, has_side_effects=True)
    every_list = (devices,) + listed.shape
    increment, area_column, totals, gathered, lists, every_seen, every_variance = pl.pallas_call(
        functools.partial(forward_kernel, devices),
        out_shape=(
            f32(cells, LANES),
            f32(latitude, LANES),
            f32(SUB, LANES),
            jax.ShapeDtypeStruct((devices, slots, LANES), jnp.bfloat16),
            jax.ShapeDtypeStruct(every_list, jnp.int32),
            f32(devices, soundings),
            f32(devices, soundings),
        ),
        in_specs=vmem(10),
        out_specs=tuple(vmem(7)),
        scratch_shapes=[
            pltpu.VMEM(blocks, jnp.float32),
            pltpu.VMEM((rows, LANES), jnp.float32),
            pltpu.VMEM(blocks, jnp.int16),
            pltpu.VMEM(blocks, jnp.int16),
            pltpu.VMEM((devices, 2 * SUB, LANES), jnp.float32),
            pltpu.VMEM((devices, 2 * SUB, LANES), jnp.float32),
            pltpu.VMEM(every_list, jnp.int32),
        ] + sems + pair + [pltpu.SemaphoreType.DMA((2 * devices,))] * 2,
        compiler_params=pltpu.CompilerParams(collective_id=0, **limits),
    )(footprint_weights.reshape(slots, LANES), listed, seen, variance, x, area_weight, time_factor, lat_factor, coarse_lon, fine_lon)

    lists = lists.reshape(-1)
    partial = pl.pallas_call(
        functools.partial(share_kernel, devices, slots, foot),
        out_shape=f32(devices, soundings),
        in_specs=smem(2) + vmem(4),
        out_specs=vmem(1)[0],
        scratch_shapes=[
            pltpu.VMEM((devices * slots, LANES), jnp.float32),
            pltpu.VMEM((cells, LANES), jnp.float32),
            pltpu.VMEM((devices * slots, LANES), jnp.float32),
        ],
        compiler_params=pltpu.CompilerParams(vmem_limit_bytes=MESH_BUDGET),
    )(lists, totals[0], gathered, increment, prior, area_weight)

    small = pltpu.VMEM((devices, SUB, LANES), jnp.float32)
    every = pl.pallas_call(
        functools.partial(misfit_kernel, devices),
        out_shape=f32(devices, soundings),
        in_specs=vmem(3),
        out_specs=vmem(1)[0],
        scratch_shapes=[pltpu.VMEM((devices, devices, soundings), jnp.float32)] + pair,
        compiler_params=pltpu.CompilerParams(collective_id=1, **limits),
    )(partial, every_seen, every_variance)

    grad = pl.pallas_call(
        functools.partial(scatter_kernel, devices, slots, foot),
        out_shape=f32(cells, LANES),
        in_specs=smem(2) + vmem(1),
        out_specs=vmem(1)[0],
        scratch_shapes=[pltpu.VMEM((devices * slots, LANES), jnp.float32)],
        compiler_params=pltpu.CompilerParams(vmem_limit_bytes=MESH_BUDGET),
    )(lists, every.reshape(-1), gathered)

    back = pl.pallas_call(
        functools.partial(adjoint_kernel, devices),
        out_shape=f32(rows, longitude),
        in_specs=vmem(7),
        out_specs=vmem(1)[0],
        scratch_shapes=[
            pltpu.VMEM(blocks, jnp.float32),
            pltpu.VMEM(blocks, jnp.float32),
            pltpu.VMEM((LANES, LANES), jnp.float32),
            pltpu.VMEM(blocks, jnp.int16),
            pltpu.VMEM(blocks, jnp.int16),
            small,
            small,
        ] + sems,
        compiler_params=pltpu.CompilerParams(collective_id=2, **limits),
    )(grad, area_column, totals, time_factor, lat_factor, coarse_lon, fine_lon)
    own = lax.dynamic_index_in_dim(every, lax.axis_index("cells"), keepdims=False)
    return control + back.reshape(control.shape), own


def fits(devices, control, coarse_lon, fine_lon, lat_factor, footprint_tiles):
    return (
        devices == coarse_lon.shape[0]
        and devices % 4 == 0
        and fine_lon.shape[0] == LANES
        and control.shape[1] == SUB
        and lat_factor.shape[0] == LANES
        and footprint_tiles.shape[0] == LANES
        and (control.shape[0] * SUB) % (16 * devices) == 0
        and control.shape[0] < LANES
        and devices * control.shape[0] * LANES * footprint_tiles.size < 2**31
        and devices < LANES
    )


def per_device(*arrays):
    devices = lax.axis_size("cells")
    control, lat_factor, coarse_lon, fine_lon, footprint_tiles = (arrays[i] for i in (0, 4, 5, 6, 7))
    if fits(devices, control, coarse_lon, fine_lon, lat_factor, footprint_tiles):
        return by_longitude(*arrays)
    return by_latitude(*arrays)


def solution(mesh):
    placed = (
        P("ens", "cells", None),
        P(None, "cells", None),
        P("cells", None),
        P(),
        P(),
        P(),
        P(),
        P("cells", None),
        P("cells", None),
        P("cells", None, None),
        P(("ens", "cells")),
        P("cells"),
    )
    return jax.shard_map(
        per_device,
        mesh=mesh,
        in_specs=placed,
        out_specs=(P("ens", "cells", None), P(("ens", "cells"))),
        check_vma=False,
    )
```
